256 devices in a mesh: dp: 32 (over y, x, core), tp: 8 (over z).
Axes of the slice: x: 4, y: 4, z: 8, core: 2. Of those that a mesh axis runs over, the one named last changes fastest.
Arguments:
- cache_keys: bfloat16 [2048, 128, 256], P('dp', 'tp'), may hold values from -6 to 6
- cache_values: bfloat16 [2048, 128, 256], P('dp', 'tp'), may hold values from -6 to 6
- page_dest: int32 [2048, 1], P('dp'), may hold values from 0 to 31; in each aligned block of 64 rows (0 to 63, 64 to 127, ...) at most 4 rows name the same one
- lengths: int32 [128], P('dp'), may hold values from 1 to 2048, 87381 in all
- queries: bfloat16 [128, 4, 4096], P('dp'), may hold values from -128 to 128
- new_keys: bfloat16 [128, 4, 256], P('dp'), may hold values from -6 to 6
- new_values: bfloat16 [128, 4, 256], P('dp'), may hold values from -6 to 6
- residual: bfloat16 [128, 4, 4096], P('dp', None, 'tp'), may hold values from -4 to 4
- out_weight: bfloat16 [4096, 4096], P(None, 'tp'), may hold values from -1 to 1
- norm_gain: float32 [4096], P('tp'), may hold values from 0.5 to 2
- expert_ids: int32 [128, 4, 8], P('dp'), may hold values from 0 to 31, all different within a row; in each aligned block of 16 rows (0 to 15, 16 to 31, ..., all dimensions but the last counted through in order) at most 6 rows name the same one
- gate_probs: float32 [128, 4, 8], P('dp'), may hold values from 0.1 to 0.6
- w_gate: bfloat16 [32, 4096, 1536], P('dp', None, 'tp'), may hold values from -0.09375 to 0.09375
- w_up: bfloat16 [32, 4096, 1536], P('dp', None, 'tp'), may hold values from -0.09375 to 0.09375
- w_down: bfloat16 [32, 1536, 4096], P('dp', 'tp'), may hold values from -0.15625 to 0.15625
Outputs:
- moved_keys: bfloat16 [4096, 128, 256], P('dp', 'tp')
- moved_values: bfloat16 [4096, 128, 256], P('dp', 'tp')
- layer_out: bfloat16 [128, 4, 4096], P('dp', None, 'tp')
The draws below stay inside these ranges and needn't reach their ends.
Inputs may be any that keep to these rules, and one draw needn't show every extreme that they name: `page_dest`: among the pages of one rank no rank is named more than 4 times. `expert_ids`: each token names 8 different experts; among the tokens of one rank no expert is named more than 6 times.
All inputs are finite; a program needn't handle non-finite values. No bound on the sum of `lengths` on one device may be relied on, other than what follows from the above.
Results may differ from the reference program's by a relative error of at most 0.02.
Values may be sent and summed in bfloat16 or wider, within the bound.
A program may use at most 64 MiB of HBM per device.

```python
import math
import jax
import jax.numpy as jnp
import numpy as np
from jax import lax

D = 4096
FF = 1536
QH = 32
KVH = 2
HEAD = 128
TOPK = 8
STEPS = 4
REQ_DEV = 4
LMAX = 2048
PAGE = 128
REQUESTS = 128
PAGES_DEV = 64
PAGES = 2048
CAPP = 4
EXPERTS = 32
CAPE = 6
N_DP = 32


def shared_keys(key):
    return jnp.clip(jax.random.normal(key, (PAGES, PAGE, KVH * HEAD), jnp.float32), -6.0, 6.0)


def draw_cache_keys(key, part):
    base_keys = shared_keys(key)
    return base_keys.astype(jnp.bfloat16)


def draw_queries(key, part):
    key = jax.random.fold_in(key, 23)
    drawn_draw = jnp.clip(jax.random.normal(key, (REQUESTS, STEPS, QH * HEAD), jnp.float32), -6.0, 6.0)
    return drawn_draw.astype(jnp.bfloat16)


def steps_of(rng, extent, cuts, smallest, high):
    gain, own = 1.0, jax.random.fold_in(rng, 6)
    for dim, blocks in cuts:
        steps = jnp.exp(jax.random.uniform(jax.random.fold_in(own, dim), (blocks,), jnp.float32, smallest / len(cuts), high / len(cuts)))
        gain = gain * jnp.repeat(steps, extent[dim] // blocks).reshape([-1 if axis == dim else 1 for axis in range(len(extent))])
    return gain


def length_profile(count, total, reach, slope):
    portions = [(1 << 20) // math.isqrt(grade ** slope) + 1 for grade in range(2, count + 1)]
    spare, counts = total - reach - (count - 1), [1] * (count - 1)
    while spare > 0:
        candidates = [i for i in range(count - 1) if counts[i] < reach]
        pool, budget = sum([portions[i] for i in candidates]), spare
        for i in candidates:
            extra = min(reach - counts[i], max(1, budget * portions[i] // pool), spare)
            counts[i] = counts[i] + extra
            spare = spare - extra
    return np.array([reach] + counts)


def ragged_sizes(key, count, total, reach, lean):
    if count == 2:
        one = jax.random.randint(key, (), max(1, total - reach), min(reach, total - 1) + 1)
        return jnp.stack([one, total - one])
    sizes = jnp.asarray(length_profile(count, total, reach, lean), jnp.int32)
    twos = (count - 1) // 2
    source_of, receiver = sizes[1:1 + 2 * twos:2], sizes[2:2 + 2 * twos:2]
    room = jnp.minimum(source_of - 1, reach - receiver)
    passed = jax.random.randint(jax.random.fold_in(key, 1), (twos,), 0, 1 << 20) % (room + 1)
    sizes = sizes.at[1:1 + 2 * twos:2].set(source_of - passed).at[2:2 + 2 * twos:2].set(receiver + passed)
    return sizes[jax.random.permutation(jax.random.fold_in(key, 2), count)]


def assign_block(rng, own, number, rows, amount, top, limit, slope):
    sequence = jax.random.permutation(rng, amount)
    packed, usual = shares(amount, rows * top, limit, slope, True), shares(amount, rows * top, limit, slope, False)
    places = jnp.arange(amount)

    def named(sizes, rotation):
        used = int((sizes > 0).sum())
        fixed = max(1, used // 4)
        moved = fixed + (places - fixed + rotation * (used - fixed)) % max(1, amount - fixed)
        return jnp.zeros((amount,), jnp.int32).at[sequence[jnp.where(places < fixed, places, moved)]].set(jnp.asarray(sizes, jnp.int32))

    sizes = jnp.where(number % 4 == 0, named(packed, number // 4), named(usual, number - number // 4 - 1))
    mixed = jax.random.permutation(jax.random.fold_in(own, 3), amount)
    giver, receiver = mixed[0:amount // 2 * 2:2], mixed[1:amount // 2 * 2:2]
    margin = jnp.minimum(sizes[giver] - 1, limit - sizes[receiver]) // 2
    margin = jnp.where((giver == sequence[0]) | (receiver == sequence[0]) | (sizes[receiver] == 0), 0, jnp.maximum(margin, 0))
    moved = jax.random.randint(jax.random.fold_in(own, 4), (amount // 2,), 0, 1 << 20) % (margin + 1)
    sizes = sizes.at[giver].add(-moved).at[receiver].add(moved)
    members = jnp.searchsorted(jnp.cumsum(sizes), jnp.arange(rows * top), side="right").astype(jnp.int32)
    grid = members.reshape(top, rows).T
    grid = grid[jax.random.permutation(jax.random.fold_in(own, 1), rows)]
    rotation = jax.random.randint(jax.random.fold_in(own, 2), (rows, 1), 0, top)
    return jnp.take_along_axis(grid, (jnp.arange(top)[None, :] + rotation) % top, axis=1)


def shares(count, total, limit, skew, full):
    weights = [(1 << 20) // math.isqrt(rank ** skew) + 1 for rank in range(1, count + 1)]
    largest = limit if full else min(limit, max(-(-total // count), total * weights[0] // sum(weights)))
    least = 1 if total - largest >= count - 1 else 0
    holding, spare = [largest] + [least] * (count - 1), total - largest - least * (count - 1)
    while spare > 0:
        free = [i for i in range(1, count) if holding[i] < largest] or [i for i in range(1, count) if holding[i] < limit]
        mass, budget = sum([weights[i] for i in free]), spare
        for i in free:
            more = min(limit - holding[i], max(1, budget * weights[i] // mass), spare)
            holding[i] = holding[i] + more
            spare = spare - more
    return np.array(holding)


def bell_draw(rng, dims, deviation, most, cuts=(), held_as=jnp.bfloat16):
    array = jax.random.normal(rng, dims, jnp.float32) * deviation
    if len(cuts) > 0:
        array = steps_of(rng, dims, cuts, -0.22, 0.18) * array
    return jnp.clip(array, min=-most, max=most).astype(held_as)


def setup_inputs(seed: int = 0) -> dict:
    streams_of = jax.random.split(jax.random.key(seed), 16)
    cache_keys = draw_cache_keys(jax.random.fold_in(streams_of[15], 71), 0)
    cache_values = bell_draw(streams_of[1], (PAGES, PAGE, KVH * HEAD), 1.0, 6.0, ((0, 32), (1, 8)))
    page_dest_keys = jax.random.split(jax.random.fold_in(streams_of[2], 1), PAGES // PAGES_DEV)
    page_dest_turns = jax.random.permutation(jax.random.fold_in(streams_of[2], 3), PAGES // PAGES_DEV)
    page_dest = jax.vmap(lambda own, number: assign_block(jax.random.fold_in(streams_of[2], 2), own, number, PAGES_DEV, N_DP, 1, CAPP, 1))(page_dest_keys, page_dest_turns).reshape((PAGES, 1))
    lengths = ragged_sizes(streams_of[3], REQUESTS, REQUESTS * LMAX // 3, LMAX, 2).astype(jnp.int32)
    queries = draw_queries(jax.random.fold_in(streams_of[15], 71), 0)
    new_keys = bell_draw(streams_of[5], (REQUESTS, STEPS, KVH * HEAD), 1.0, 6.0, ((0, 32),))
    new_values = bell_draw(streams_of[6], (REQUESTS, STEPS, KVH * HEAD), 1.0, 6.0, ((0, 32),))
    residual = bell_draw(streams_of[7], (REQUESTS, STEPS, D), 0.3, 4.0, ((0, 32), (2, 8)))
    out_weight = bell_draw(streams_of[8], (QH * HEAD, D), (4.0 / (QH * HEAD) ** 0.5), 1.0, ((1, 8),))
    norm_gain = jnp.clip(jnp.exp(math.log(2.0) - 1.3862944 * jax.random.uniform(streams_of[9], (D,), jnp.float32) ** steps_of(streams_of[9], (D,), ((0, 8),), -0.2, 0.2)), 0.5, 2.0)
    expert_ids_keys = jax.random.split(jax.random.fold_in(streams_of[10], 1), REQUESTS * STEPS // (REQ_DEV * STEPS))
    expert_ids_turns = jax.random.permutation(jax.random.fold_in(streams_of[10], 3), REQUESTS * STEPS // (REQ_DEV * STEPS))
    expert_ids = jax.vmap(lambda own, number: assign_block(jax.random.fold_in(streams_of[10], 2), own, number, REQ_DEV * STEPS, EXPERTS, TOPK, CAPE, 2))(expert_ids_keys, expert_ids_turns).reshape((REQUESTS, STEPS, TOPK))
    gate_probs = jnp.clip(0.1 + 0.5 * jax.random.uniform(streams_of[11], (REQUESTS, STEPS, TOPK), jnp.float32) ** steps_of(streams_of[11], (REQUESTS, STEPS, TOPK), ((0, 32),), -0.2, 0.2), 0.1, 0.6)
    w_gate = bell_draw(streams_of[12], (EXPERTS, D, FF), D ** -0.5, 0.09375, ((0, 32), (2, 8)))
    w_up = bell_draw(streams_of[13], (EXPERTS, D, FF), D ** -0.5, 0.09375, ((0, 32), (2, 8)))
    w_down = bell_draw(streams_of[14], (EXPERTS, FF, D), FF ** -0.5, 0.15625, ((0, 32), (1, 8)))
    return dict(cache_keys=cache_keys, cache_values=cache_values, page_dest=page_dest, lengths=lengths, queries=queries, new_keys=new_keys, new_values=new_values, residual=residual, out_weight=out_weight, norm_gain=norm_gain, expert_ids=expert_ids, gate_probs=gate_probs, w_gate=w_gate, w_up=w_up, w_down=w_down)


EPSILON = 1e-06

def slot_ranks(groups, count_to):
    onehot = (groups[..., None] == jnp.arange(count_to, dtype=jnp.int32)).astype(jnp.int32)
    before = jnp.cumsum(onehot, axis=1) - onehot
    return lax.optimization_barrier(jnp.sum(before * onehot, axis=-1)).astype(jnp.int32)

def migrate(pages, page_dest):
    target = page_dest[:, 0].reshape(N_DP, PAGES_DEV)
    within = slot_ranks(target, N_DP)
    source = jnp.arange(N_DP, dtype=jnp.int32)[:, None]
    where_to = (target * (N_DP * CAPP) + source * CAPP + within).reshape(-1)
    out_shape = (N_DP * N_DP * CAPP,) + pages.shape[1:]
    return jnp.zeros(out_shape, pages.dtype).at[where_to].set(pages)

def attend_one(request_data):
    req_keys, req_values, length, query_rows, fresh_keys, fresh_values = request_data
    group_size = QH // KVH
    all_keys = jnp.concatenate([req_keys, fresh_keys], 0).astype(jnp.float32).reshape(LMAX + STEPS, KVH, HEAD)
    all_values = jnp.concatenate([req_values, fresh_values], 0).astype(jnp.float32).reshape(LMAX + STEPS, KVH, HEAD)
    query_heads = query_rows.astype(jnp.float32).reshape(STEPS, KVH, group_size, HEAD)
    score_scale = 1.0 / math.sqrt(HEAD)
    scores = jnp.einsum('skgd,pkd->skgp', query_heads, all_keys, precision=lax.Precision.HIGHEST) * score_scale
    position = jnp.arange(LMAX + STEPS, dtype=jnp.int32)[None, :]
    step_ids = jnp.arange(STEPS, dtype=jnp.int32)[:, None]
    visible = jnp.where(position < LMAX, position < length, position - LMAX <= step_ids)
    visible = visible[:, None, None, :]
    scores = jnp.where(visible, scores, -1e+30)
    top_score = lax.optimization_barrier(jnp.max(scores, axis=-1, keepdims=True))
    weights = jnp.where(visible, jnp.exp(scores - top_score), 0.0)
    weight_sum = lax.optimization_barrier(jnp.sum(weights, axis=-1))
    value_sum = jnp.einsum('skgp,pkd->skgd', weights, all_values, precision=lax.Precision.HIGHEST)
    return (value_sum / weight_sum[..., None]).reshape(STEPS, QH * HEAD).astype(jnp.bfloat16)

def run_expert(expert_data):
    in_rows, gate_matrix, up_matrix, down_matrix = expert_data
    gate_part = jnp.dot(in_rows, gate_matrix, preferred_element_type=jnp.float32)
    up_part = jnp.dot(in_rows, up_matrix, preferred_element_type=jnp.float32)
    hidden = (jax.nn.silu(gate_part) * up_part).astype(jnp.bfloat16)
    return jnp.dot(hidden, down_matrix, preferred_element_type=jnp.float32).astype(jnp.bfloat16)

def reference(cache_keys, cache_values, page_dest, lengths, queries, new_keys, new_values, residual, out_weight, norm_gain, expert_ids, gate_probs, w_gate, w_up, w_down):
    moved_keys = migrate(cache_keys, page_dest)
    moved_values = migrate(cache_values, page_dest)
    req_keys = cache_keys.reshape(REQUESTS, LMAX, KVH * HEAD)
    req_values = cache_values.reshape(REQUESTS, LMAX, KVH * HEAD)
    attended = lax.map(attend_one, (req_keys, req_values, lengths, queries, new_keys, new_values))
    projected = jnp.dot(attended.reshape(-1, QH * HEAD), out_weight, preferred_element_type=jnp.float32)
    projected = projected.reshape(REQUESTS, STEPS, D)
    layer_state = (residual.astype(jnp.float32) + projected).astype(jnp.bfloat16)
    state_wide = layer_state.astype(jnp.float32)
    mean_square = lax.optimization_barrier(jnp.mean(jnp.square(state_wide), axis=-1, keepdims=True))
    normed = (state_wide * lax.rsqrt(mean_square + EPSILON) * norm_gain.astype(jnp.float32)).astype(jnp.bfloat16)
    flat_ids = expert_ids.reshape(N_DP, REQ_DEV * STEPS * TOPK)
    within = slot_ranks(flat_ids, EXPERTS)
    source = jnp.arange(N_DP, dtype=jnp.int32)[:, None]
    row_index = (source * CAPE + within).reshape(-1)
    expert_index = flat_ids.reshape(-1)
    token_rows = jnp.repeat(normed.reshape(-1, D), TOPK, axis=0)
    buffers = jnp.zeros((EXPERTS, N_DP * CAPE, D), jnp.bfloat16).at[expert_index, row_index].set(token_rows)
    finished = lax.map(run_expert, (buffers, w_gate, w_up, w_down))
    picked = finished[expert_index, row_index].reshape(REQUESTS, STEPS, TOPK, D).astype(jnp.float32)
    mixture = jnp.einsum('rsk,rskd->rsd', gate_probs.astype(jnp.float32), picked, precision=lax.Precision.HIGHEST)
    layer_out = (state_wide + mixture).astype(jnp.bfloat16)
    return (moved_keys, moved_values, layer_out)
```

```python
import math

import jax
import jax.numpy as jnp
from jax import lax
from jax.experimental import pallas as pl
from jax.experimental.pallas import tpu as pltpu
from jax.sharding import PartitionSpec as P

MESH = pl.DeviceIdType.MESH
F32 = jnp.float32
BF16 = jnp.bfloat16

DP = 32
TP = 8
HEAD = 128
TOKENS = 16
SLOTS = 6
PAD_SLOTS = 8
ROWS = DP * SLOTS
HALF = ROWS // 2
PART = 512
WIDE = 256
BLOCK = 16
EPSILON = 1e-06
LOW = -1e30


def iota(shape, dim):
    return lax.broadcasted_iota(jnp.int32, shape, dim)


def onehot(mask):
    return jnp.where(mask, 1.0, 0.0).astype(BF16)


def dot(a, b):
    return jnp.dot(a, b, preferred_element_type=F32)


def dot_last(a, b):
    return lax.dot_general(a, b, (((1,), (1,)), ((), ())), preferred_element_type=F32)


def split_three(value):
    top = value.astype(BF16).astype(F32)
    rest = value - top
    middle = rest.astype(BF16).astype(F32)
    return top, middle, rest - middle


def layer_kernel(
    inverse, lengths, queries, new_keys, new_values, residual, gain, scatter, gather,
    keys, values, out_weight, w_gate, w_up, w_down,
    moved_keys, moved_values, layer_out,
    kbuf, vbuf, ksend, vsend, wo, wg, wu, wd,
    part_send, part_recv, coeff, attended, state,
    disp_send, disp_recv, xbuf, sqbuf, gate_acc, up_acc, ybuf,
    lsend, rsend, lrecv, rrecv, ret_send, ret_recv,
    local_sem, page_send_sem, page_recv_sem, part_ssem, part_rsem, att_ssem, att_rsem,
    disp_ssem, disp_rsem, sq_ssem, sq_rsem, ring_ssem, ring_rsem, red_ssem, red_rsem,
    ret_ssem, ret_rsem,
):
    me = lax.axis_index("dp")
    t = lax.axis_index("tp")

    def local(src, dst, i):
        return pltpu.make_async_copy(src, dst, local_sem.at[i])

    loads = [
        local(keys, kbuf.at[pl.ds(0, 64)], 0),
        local(values, vbuf.at[pl.ds(0, 64)], 1),
        local(out_weight, wo, 2),
        local(w_gate, wg, 3),
        local(w_up, wu, 4),
        local(w_down, wd, 5),
    ]
    for load in loads:
        load.start()

    barrier = pltpu.get_barrier_semaphore()

    @pl.loop(1, DP)
    def _(d):
        pl.semaphore_signal(
            barrier, inc=1, device_id=(lax.rem(me + d, DP), t), device_id_type=MESH
        )

    for d in range(1, TP):
        pl.semaphore_signal(
            barrier, inc=1, device_id=(me, lax.rem(t + d, TP)), device_id_type=MESH
        )

    kbuf[64] = jnp.zeros((16, WIDE), BF16)
    vbuf[64] = jnp.zeros((16, WIDE), BF16)
    loads[0].wait()
    loads[1].wait()

    row = iota((256, 256), 0)
    col = iota((256, 256), 1)
    perm = onehot(col == ((row >> 2) & 15) * 16 + (row >> 6) * 4 + (row & 3))
    perm_back = onehot(col == ((row >> 2) & 3) * 64 + (row >> 4) * 4 + (row & 3))
    scale = 1.0 / math.sqrt(HEAD)
    lane = iota((64, 256), 1)
    position = (lane >> 4) * 128 + t * 16 + (lane & 15)
    frow = iota((64, TOKENS), 0)
    fcol = iota((64, TOKENS), 1)
    stat_lane = iota((256, HEAD), 1)
    for k in range(2):
        cols = slice(k * HEAD, (k + 1) * HEAD)
        q_rows = jnp.concatenate(
            [queries[:, (k * 16 + g) * HEAD : (k * 16 + g + 1) * HEAD] for g in range(16)], axis=0
        )
        q_rows = dot(perm, q_rows).astype(BF16)
        fresh_k = new_keys[:, cols]
        fresh_v = new_values[:, cols]
        accs, tops, sums = [], [], []
        for r in range(4):
            k_r = kbuf[16 * r : 16 * r + 16].reshape(256, WIDE)[:, cols]
            v_r = vbuf[16 * r : 16 * r + 16].reshape(256, WIDE)[:, cols]
            q_r = q_rows[64 * r : 64 * r + 64]
            visible = position < lengths[r]
            scores = jnp.where(visible, dot_last(q_r, k_r) * scale, LOW)
            fvisible = ((fcol >> 2) == r) & ((fcol & 3) <= (frow & 3)) & (t == 0)
            fscores = jnp.where(fvisible, dot_last(q_r, fresh_k) * scale, LOW)
            top = jnp.maximum(
                jnp.max(scores, axis=1, keepdims=True), jnp.max(fscores, axis=1, keepdims=True)
            )
            weights = jnp.where(visible, jnp.exp(scores - top), 0.0)
            fweights = jnp.where(fvisible, jnp.exp(fscores - top), 0.0)
            sums.append(
                jnp.sum(weights, axis=1, keepdims=True) + jnp.sum(fweights, axis=1, keepdims=True)
            )
            tops.append(top)
            accs.append(dot(weights.astype(BF16), v_r) + dot(fweights.astype(BF16), fresh_v))
        acc = dot(perm_back, jnp.concatenate(accs, axis=0).astype(BF16)).astype(BF16)
        stats = jnp.zeros((256, HEAD), F32)
        pieces = split_three(jnp.concatenate(tops, axis=0)) + split_three(
            jnp.concatenate(sums, axis=0)
        )
        for i, piece in enumerate(pieces):
            stats = jnp.where(stat_lane == i, piece, stats)
        stats = jnp.transpose(stats)[0:16].astype(BF16)
        stats = dot(stats, perm).astype(BF16)
        for q in range(4):
            part_send[k * 4 + q, 0:64] = acc[64 * q : 64 * q + 64]
            part_send[k * 4 + q, 64:80] = stats[:, 128 * (q >> 1) : 128 * (q >> 1) + 128]

    pl.semaphore_wait(barrier, DP - 1 + TP - 1)

    def part_copy(d):
        dest = lax.rem(t + d, TP)
        return pltpu.make_async_remote_copy(
            src_ref=part_send.at[dest],
            dst_ref=part_recv.at[t],
            send_sem=part_ssem.at[d],
            recv_sem=part_rsem.at[t],
            device_id=(me, dest),
            device_id_type=MESH,
        )

    for d in range(1, TP):
        part_copy(d).start()
    part_recv[t] = part_send[t]

    @pl.loop(0, 128)
    def _(slot):
        page = inverse[slot]
        ksend[slot] = kbuf[page]
        vsend[slot] = vbuf[page]

    def page_copy(which, d):
        dest = lax.rem(me + d, DP)
        src, dst = ((ksend, moved_keys), (vsend, moved_values))[which]
        return pltpu.make_async_remote_copy(
            src_ref=src.at[pl.ds(dest * 4, 4)],
            dst_ref=dst.at[pl.ds(me * 4, 4)],
            send_sem=page_send_sem.at[which, dest],
            recv_sem=page_recv_sem.at[which, me],
            device_id=(dest, t),
            device_id_type=MESH,
        )

    @pl.loop(1, DP)
    def _(d):
        page_copy(0, d).start()
        page_copy(1, d).start()

    own_k = local(ksend.at[pl.ds(me * 4, 4)], moved_keys.at[pl.ds(me * 4, 4)], 6)
    own_v = local(vsend.at[pl.ds(me * 4, 4)], moved_values.at[pl.ds(me * 4, 4)], 7)
    own_k.start()
    own_v.start()

    def wait_recv(ref, sem):
        pltpu.make_async_copy(ref, ref, sem).wait()

    for d in range(1, TP):
        src = lax.rem(t + d, TP)
        wait_recv(part_recv.at[src], part_rsem.at[src])
    tops, sums = [], []
    for s in range(TP):
        stat = part_recv[s, 64:80].astype(F32)
        tops.append(stat[0:1] + stat[1:2] + stat[2:3])
        sums.append(stat[3:4] + stat[4:5] + stat[5:6])
    tops = jnp.concatenate(tops, axis=0)
    sums = jnp.concatenate(sums, axis=0)
    scales = jnp.exp(tops - jnp.max(tops, axis=0, keepdims=True))
    scales = scales / jnp.sum(scales * sums, axis=0, keepdims=True)
    scales = jnp.concatenate([scales, jnp.zeros((120, HEAD), F32)], axis=0)
    coeff[...] = jnp.transpose(scales)
    mine = coeff[pl.ds(pl.multiple_of((t & 1) * 64, 64), 64), :]
    merged = jnp.zeros((64, HEAD), F32)
    for s in range(TP):
        merged = merged + mine[:, s : s + 1] * part_recv[s, 0:64].astype(F32)
    merged = merged.astype(BF16)
    for h in range(4):
        attended[t, :, h * HEAD : (h + 1) * HEAD] = merged[h * 16 : h * 16 + 16]

    def att_copy(d):
        return pltpu.make_async_remote_copy(
            src_ref=attended.at[t],
            dst_ref=attended.at[t],
            send_sem=att_ssem.at[d],
            recv_sem=att_rsem.at[t],
            device_id=(me, lax.rem(t + d, TP)),
            device_id_type=MESH,
        )

    for d in range(1, TP):
        att_copy(d).start()

    loads[2].wait()

    def project(src):
        return dot(attended[src], wo[pl.ds(pl.multiple_of(src * PART, PART), PART), :])

    projected = project(t)
    for d in (1, 7, 2, 6, 3, 5, 4):
        src = lax.rem(t + d, TP)
        wait_recv(attended.at[src], att_rsem.at[src])
        projected = projected + project(src)
    layer_state = (residual[...].astype(F32) + projected).astype(BF16)
    state[...] = layer_state

    stacked = jnp.concatenate([layer_state[:, :WIDE], layer_state[:, WIDE:]], axis=0)
    disp_send[...] = dot(scatter[...], stacked).astype(BF16)

    def block_of(ref, rank):
        return ref.at[pl.ds(pl.multiple_of(rank * BLOCK, BLOCK), BLOCK)]

    def all_copy(send, recv, ssem, rsem, d):
        dest = lax.rem(me + d, DP)
        return pltpu.make_async_remote_copy(
            src_ref=block_of(send, dest),
            dst_ref=block_of(recv, me),
            send_sem=ssem.at[dest],
            recv_sem=rsem.at[me],
            device_id=(dest, t),
            device_id_type=MESH,
        )

    def exchange(send, recv, ssem, rsem):
        @pl.loop(1, DP)
        def _(d):
            all_copy(send, recv, ssem, rsem, d).start()

        block = pl.ds(pl.multiple_of(me * BLOCK, BLOCK), BLOCK)
        recv[block, :] = send[block, :]

        @pl.loop(1, DP)
        def _(d):
            src = lax.rem(me + d, DP)
            wait_recv(block_of(recv, src), rsem.at[src])

    exchange(disp_send, disp_recv, disp_ssem, disp_rsem)

    prow = iota((ROWS, DP * BLOCK), 0)
    pcol = iota((ROWS, DP * BLOCK), 1)
    place = (prow & 31) * BLOCK + (prow >> 5)
    arrived = disp_recv[...]
    square = jnp.zeros((ROWS, 1), F32)
    for h in range(2):
        piece = dot(onehot(pcol == place + h * PAD_SLOTS), arrived)
        square = square + jnp.sum(piece * piece, axis=1, keepdims=True)
        xbuf[t, :, h * WIDE : (h + 1) * WIDE] = (
            piece * gain[:, h * WIDE : (h + 1) * WIDE]
        ).astype(BF16)
    square = jnp.concatenate([square, jnp.zeros((256 - ROWS, 1), F32)], axis=0)
    sqbuf[t] = jnp.transpose(jnp.broadcast_to(square, (256, HEAD)))[0:1]

    def sq_copy(d):
        return pltpu.make_async_remote_copy(
            src_ref=sqbuf.at[t],
            dst_ref=sqbuf.at[t],
            send_sem=sq_ssem.at[d],
            recv_sem=sq_rsem.at[t],
            device_id=(me, lax.rem(t + d, TP)),
            device_id_type=MESH,
        )

    for d in range(1, TP):
        sq_copy(d).start()

    toward = (lax.rem(t + 1, TP), lax.rem(t + TP - 1, TP))

    def rows_of(sub):
        return pl.ds(sub * HALF, HALF)

    def ring_copy(way, i):
        step = i // 2
        chunk = lax.rem(t + (TP - step if way == 0 else step), TP)
        piece = xbuf.at[chunk, rows_of((i + way) % 2)]
        return pltpu.make_async_remote_copy(
            src_ref=piece,
            dst_ref=piece,
            send_sem=ring_ssem.at[way, i],
            recv_sem=ring_rsem.at[way, i],
            device_id=(me, toward[way]),
            device_id_type=MESH,
        )

    def ring_wait(way, i):
        step = i // 2 + 1
        chunk = lax.rem(t + (TP - step if way == 0 else step), TP)
        wait_recv(xbuf.at[chunk, rows_of((i + way) % 2)], ring_rsem.at[way, i])

    def expert_in(chunk, first=False):
        x = xbuf[chunk]
        weight_rows = pl.ds(pl.multiple_of(chunk * PART, PART), PART)
        gate_part = dot(x, wg[weight_rows, :])
        up_part = dot(x, wu[weight_rows, :])
        if first:
            gate_acc[...] = gate_part
            up_acc[...] = up_part
        else:
            gate_acc[...] += gate_part
            up_acc[...] += up_part

    for i in range(2):
        for way in range(2):
            ring_copy(way, i).start()
    loads[3].wait()
    loads[4].wait()
    expert_in(t, first=True)
    for i in range(7):
        for way in range(2):
            ring_wait(way, i)
            if i + 2 < 7:
                ring_copy(way, i + 2).start()
        if i % 2 == 1:
            expert_in(lax.rem(t + TP - (i // 2 + 1), TP))
            expert_in(lax.rem(t + i // 2 + 1, TP))
    expert_in(lax.rem(t + 4, TP))

    for d in range(1, TP):
        src = lax.rem(t + d, TP)
        wait_recv(sqbuf.at[src], sq_rsem.at[src])
    total = sqbuf[0]
    for s in range(1, TP):
        total = total + sqbuf[s]
    inv_norm = lax.rsqrt(total * (1.0 / (TP * PART)) + EPSILON)
    inv_norm = jnp.transpose(jnp.broadcast_to(inv_norm, (HEAD, 256)))[0:ROWS, 0:1]
    gate_part = gate_acc[...] * inv_norm
    up_part = up_acc[...] * inv_norm
    hidden = (gate_part / (1.0 + jnp.exp(-gate_part)) * up_part).astype(BF16)

    loads[5].wait()
    sends = (rsend, lsend)
    recvs = (rrecv, lrecv)

    def expert_out(chunk):
        ybuf[chunk] = dot(hidden, wd[:, pl.ds(pl.multiple_of(chunk * PART, PART), PART)])

    def red_copy(way, j):
        return pltpu.make_async_remote_copy(
            src_ref=sends[way].at[j],
            dst_ref=recvs[way].at[j],
            send_sem=red_ssem.at[way, j],
            recv_sem=red_rsem.at[way, j],
            device_id=(me, toward[way]),
            device_id_type=MESH,
        )

    for j in range(7):
        for way in range(2):
            distance = 4 - (j + 1) // 2
            chunk = lax.rem(t + (distance if way == 0 else TP - distance), TP)
            sub = (j + 1 + way) % 2
            if j == 0:
                if way == 0:
                    expert_out(chunk)
            elif j % 2 == 1:
                expert_out(chunk)
            value = ybuf[chunk, sub * HALF : (sub + 1) * HALF]
            if j >= 2:
                wait_recv(recvs[way].at[j - 2], red_rsem.at[way, j - 2])
                value = value + recvs[way][j - 2].astype(F32)
            sends[way][j] = value.astype(BF16)
            red_copy(way, j).start()
    expert_out(t)
    for j in (5, 6):
        for way in range(2):
            wait_recv(recvs[way].at[j], red_rsem.at[way, j])
    results = []
    for sub in range(2):
        value = ybuf[t, sub * HALF : (sub + 1) * HALF]
        value = value + recvs[0][5 + sub].astype(F32)
        value = value + recvs[1][6 - sub].astype(F32)
        results.append(value.astype(BF16))
    result = jnp.concatenate(results, axis=0)

    rrow = iota((DP * BLOCK, ROWS), 0)
    rcol = iota((DP * BLOCK, ROWS), 1)
    rplace = (rrow & 7) * DP + (rrow >> 4)
    back = jnp.zeros((DP * BLOCK, WIDE), F32)
    for h in range(2):
        pick = onehot((rcol == rplace) & (((rrow >> 3) & 1) == h))
        back = back + dot(pick, result[:, h * WIDE : (h + 1) * WIDE])
    ret_send[...] = back.astype(BF16)
    exchange(ret_send, ret_recv, ret_ssem, ret_rsem)

    weights = gather[...]
    weights_top = weights.astype(BF16)
    weights_rest = (weights - weights_top.astype(F32)).astype(BF16)
    returned = ret_recv[...]
    mixture = dot(weights_top, returned) + dot(weights_rest, returned)
    for h in range(2):
        features = slice(h * WIDE, (h + 1) * WIDE)
        layer_out[:, features] = (
            state[:, features].astype(F32) + mixture[h * TOKENS : (h + 1) * TOKENS]
        ).astype(BF16)

    own_k.wait()
    own_v.wait()

    @pl.loop(1, DP)
    def _(d):
        src = lax.rem(me + d, DP)
        dst = pl.ds(src * 4, 4)
        wait_recv(moved_keys.at[dst], page_recv_sem.at[0, src])
        wait_recv(moved_values.at[dst], page_recv_sem.at[1, src])
        page_copy(0, d).wait_send()
        page_copy(1, d).wait_send()
        all_copy(disp_send, disp_recv, disp_ssem, disp_rsem, d).wait_send()
        all_copy(ret_send, ret_recv, ret_ssem, ret_rsem, d).wait_send()

    for d in range(1, TP):
        part_copy(d).wait_send()
        att_copy(d).wait_send()
        sq_copy(d).wait_send()
    for i in range(7):
        for way in range(2):
            ring_copy(way, i).wait_send()
            red_copy(way, i).wait_send()


def layer(inverse, lengths, queries, new_keys, new_values, residual, gain, scatter, gather,
          keys, values, out_weight, w_gate, w_up, w_down):
    smem = pl.BlockSpec(memory_space=pltpu.SMEM)
    vmem = pl.BlockSpec(memory_space=pltpu.VMEM)
    hbm = pl.BlockSpec(memory_space=pl.ANY)
    dma = pltpu.SemaphoreType.DMA
    return pl.pallas_call(
        layer_kernel,
        out_shape=(
            jax.ShapeDtypeStruct((128, 16, WIDE), BF16),
            jax.ShapeDtypeStruct((128, 16, WIDE), BF16),
            jax.ShapeDtypeStruct((TOKENS, PART), BF16),
        ),
        in_specs=[smem, smem] + [vmem] * 7 + [hbm] * 6,
        out_specs=(hbm, hbm, vmem),
        scratch_shapes=[
            pltpu.VMEM((65, 16, WIDE), BF16),
            pltpu.VMEM((65, 16, WIDE), BF16),
            pltpu.VMEM((128, 16, WIDE), BF16),
            pltpu.VMEM((128, 16, WIDE), BF16),
            pltpu.VMEM((4096, PART), BF16),
            pltpu.VMEM((4096, 192), BF16),
            pltpu.VMEM((4096, 192), BF16),
            pltpu.VMEM((192, 4096), BF16),
            pltpu.VMEM((TP, 80, HEAD), BF16),
            pltpu.VMEM((TP, 80, HEAD), BF16),
            pltpu.VMEM((HEAD, HEAD), F32),
            pltpu.VMEM((TP, TOKENS, PART), BF16),
            pltpu.VMEM((TOKENS, PART), BF16),
            pltpu.VMEM((DP * BLOCK, WIDE), BF16),
            pltpu.VMEM((DP * BLOCK, WIDE), BF16),
            pltpu.VMEM((TP, ROWS, PART), BF16),
            pltpu.VMEM((TP, 1, 256), F32),
            pltpu.VMEM((ROWS, 192), F32),
            pltpu.VMEM((ROWS, 192), F32),
            pltpu.VMEM((TP, ROWS, PART), F32),
            pltpu.VMEM((7, HALF, PART), BF16),
            pltpu.VMEM((7, HALF, PART), BF16),
            pltpu.VMEM((7, HALF, PART), BF16),
            pltpu.VMEM((7, HALF, PART), BF16),
            pltpu.VMEM((DP * BLOCK, WIDE), BF16),
            pltpu.VMEM((DP * BLOCK, WIDE), BF16),
            dma((8,)),
            dma((2, DP)), dma((2, DP)),
            dma((TP,)), dma((TP,)), dma((TP,)), dma((TP,)),
            dma((DP,)), dma((DP,)),
            dma((TP,)), dma((TP,)),
            dma((2, 7)), dma((2, 7)), dma((2, 7)), dma((2, 7)),
            dma((DP,)), dma((DP,)),
        ],
        compiler_params=pltpu.CompilerParams(
            collective_id=0, has_side_effects=True, vmem_limit_bytes=48 * 1024 * 1024
        ),
    )(inverse, lengths, queries, new_keys, new_values, residual, gain, scatter, gather,
      keys, values, out_weight, w_gate, w_up, w_down)


def shards(
    cache_keys, cache_values, page_dest, lengths, queries, new_keys, new_values, residual,
    out_weight, norm_gain, expert_ids, gate_probs, w_gate, w_up, w_down,
):
    target = page_dest[:, 0]
    number = jnp.arange(64, dtype=jnp.int32)
    earlier = (target[:, None] == target[None, :]) & (number[None, :] < number[:, None])
    within = jnp.sum(earlier.astype(jnp.int32), axis=1)
    slot = target * 4 + within
    hit = slot[None, :] == jnp.arange(128, dtype=jnp.int32)[:, None]
    inverse = 64 + jnp.sum(jnp.where(hit, number[None, :] - 64, 0), axis=1)

    ids = expert_ids.reshape(TOKENS, -1)
    probs = gate_probs.reshape(TOKENS, -1)
    named = ids[:, :, None] == jnp.arange(DP, dtype=jnp.int32)
    member = jnp.any(named, axis=1)
    weight = jnp.sum(jnp.where(named, probs[:, :, None], 0.0), axis=1)
    token = jnp.arange(TOKENS, dtype=jnp.int32)
    before = jnp.where(token[None, :] < token[:, None], 1, 0)
    rank = jnp.sum(before[:, :, None] * member.astype(jnp.int32)[None], axis=1)
    slots = jnp.arange(PAD_SLOTS, dtype=jnp.int32)
    chosen = (member[:, :, None] & (rank[:, :, None] == slots)).astype(F32)
    halves = jnp.eye(2, dtype=F32)
    scatter = (
        chosen.transpose(1, 2, 0)[:, None, :, None, :] * halves[None, :, None, :, None]
    ).reshape(DP * BLOCK, 2 * TOKENS).astype(BF16)
    gather = (
        (chosen * weight[:, :, None])[None, :, :, None, :] * halves[:, None, None, :, None]
    ).reshape(2 * TOKENS, DP * BLOCK)

    moved_keys, moved_values, layer_out = layer(
        inverse,
        lengths,
        queries.reshape(TOKENS, -1),
        new_keys.reshape(TOKENS, -1),
        new_values.reshape(TOKENS, -1),
        residual.reshape(TOKENS, -1),
        norm_gain[None, :],
        scatter,
        gather,
        cache_keys,
        cache_values,
        out_weight,
        w_gate[0],
        w_up[0],
        w_down[0],
    )
    return moved_keys, moved_values, layer_out.reshape(residual.shape)


def solution(mesh):
    in_specs = (
        P("dp", "tp", None),
        P("dp", "tp", None),
        P("dp", None),
        P("dp"),
        P("dp", None, None),
        P("dp", None, None),
        P("dp", None, None),
        P("dp", None, "tp"),
        P(None, "tp"),
        P("tp"),
        P("dp", None, None),
        P("dp", None, None),
        P("dp", None, "tp"),
        P("dp", None, "tp"),
        P("dp", "tp", None),
    )
    out_specs = (P("dp", "tp", None), P("dp", "tp", None), P("dp", None, "tp"))
    return jax.shard_map(shards, mesh=mesh, in_specs=in_specs, out_specs=out_specs, check_vma=False)
```

```python
import math

import jax
import jax.numpy as jnp
from jax import lax
from jax.experimental import pallas as pl
from jax.experimental.pallas import tpu as pltpu
from jax.sharding import PartitionSpec as P

MESH = pl.DeviceIdType.MESH
F32 = jnp.float32
BF16 = jnp.bfloat16

DP = 32
TP = 8
HEAD = 128
TOKENS = 16
SLOTS = 6
PAD_SLOTS = 8
ROWS = DP * SLOTS
SUBS = 4
SUB_ROWS = ROWS // SUBS
MESSAGES = 7 * SUBS // 2
PART = 512
WIDE = 256
BLOCK = 16
EPSILON = 1e-06
LOW = -1e30
EARLY = 10


def iota(shape, dim):
    return lax.broadcasted_iota(jnp.int32, shape, dim)


def onehot(mask):
    return jnp.where(mask, 1.0, 0.0).astype(BF16)


def dot(a, b):
    return jnp.dot(a, b, preferred_element_type=F32)


def dot_last(a, b):
    return lax.dot_general(a, b, (((1,), (1,)), ((), ())), preferred_element_type=F32)


def split_three(value):
    top = value.astype(BF16).astype(F32)
    rest = value - top
    middle = rest.astype(BF16).astype(F32)
    return top, middle, rest - middle


def layer_kernel(
    lengths, page_dest_in, queries_in, new_keys_in, new_values_in, residual_in, gain_in, ids_in,
    probs_in, keys, values, out_weight, w_gate, w_up, w_down,
    moved_keys, moved_values, layer_out,
    page_dest, queries, new_keys, new_values, residual, gain, ids, probs,
    qrows, idrows, new_rows, inverse_row, inverse, pick_in, pick_out,
    kbuf, vbuf, ksend, vsend, wo, wg, wu, wd,
    part_send, part_recv, coeff, attended, state,
    disp_send, disp_recv, xbuf, sqbuf, gate_acc, up_acc, ybuf,
    lsend, rsend, lrecv, rrecv, ret_send, ret_recv,
    local_sem, page_send_sem, page_recv_sem, part_ssem, part_rsem, att_ssem, att_rsem,
    disp_ssem, disp_rsem, sq_ssem, sq_rsem, ring_ssem, ring_rsem, red_ssem, red_rsem,
    ret_ssem, ret_rsem,
):
    me = lax.axis_index("dp")
    t = lax.axis_index("tp")

    def local(src, dst, i):
        return pltpu.make_async_copy(src, dst, local_sem.at[i])

    small = [
        local(src, dst, 8 + i)
        for i, (src, dst) in enumerate((
            (page_dest_in, page_dest), (queries_in, queries), (new_keys_in, new_keys),
            (new_values_in, new_values), (residual_in, residual), (gain_in, gain),
            (ids_in, ids), (probs_in, probs),
        ))
    ]
    loads = [
        local(keys, kbuf.at[pl.ds(0, 64)], 0),
        local(values, vbuf.at[pl.ds(0, 64)], 1),
        local(out_weight, wo, 2),
        local(w_gate, wg, 3),
        local(w_up, wu, 4),
        local(w_down, wd, 5),
    ]
    for load in small + loads:
        load.start()

    barrier = pltpu.get_barrier_semaphore()

    @pl.loop(1, DP)
    def _(d):
        pl.semaphore_signal(
            barrier, inc=1, device_id=(lax.rem(me + d, DP), t), device_id_type=MESH
        )

    for d in range(1, TP):
        pl.semaphore_signal(
            barrier, inc=1, device_id=(me, lax.rem(t + d, TP)), device_id_type=MESH
        )

    kbuf[64] = jnp.zeros((16, WIDE), BF16)
    vbuf[64] = jnp.zeros((16, WIDE), BF16)
    for load in small:
        load.wait()

    def rows_together(ref, scratch):
        for r in range(4):
            scratch[4 * r : 4 * r + 4, : ref.shape[2]] = ref[r].astype(F32)
        return scratch[:, : ref.shape[2]]

    rows_together(new_keys, new_rows.at[0])
    rows_together(new_values, new_rows.at[1])
    residual_rows = rows_together(residual, idrows)
    rows_together(queries, qrows)

    loads[0].wait()
    loads[1].wait()

    row = iota((256, 256), 0)
    col = iota((256, 256), 1)
    perm = onehot(col == ((row >> 2) & 15) * 16 + (row >> 6) * 4 + (row & 3))
    perm_back = onehot(col == ((row >> 2) & 3) * 64 + (row >> 4) * 4 + (row & 3))
    scale = 1.0 / math.sqrt(HEAD)
    lane = iota((64, 256), 1)
    position = (lane >> 4) * 128 + t * 16 + (lane & 15)
    frow = iota((256, TOKENS), 0)
    fcol = iota((256, TOKENS), 1)
    fvisible = ((fcol >> 2) == (frow >> 6)) & ((fcol & 3) <= (frow & 3)) & (t == 0)
    stat_lane = iota((256, HEAD), 1)

    def part_copy(d):
        dest = lax.rem(t + d, TP)
        return pltpu.make_async_remote_copy(
            src_ref=part_send.at[dest],
            dst_ref=part_recv.at[t],
            send_sem=part_ssem.at[d],
            recv_sem=part_rsem.at[t],
            device_id=(me, dest),
            device_id_type=MESH,
        )

    def attend(k):
        cols = pl.ds(pl.multiple_of(k * HEAD, HEAD), HEAD)
        q_rows = jnp.concatenate(
            [
                qrows[:, pl.ds(pl.multiple_of((k * 16 + g) * HEAD, HEAD), HEAD)]
                for g in range(16)
            ],
            axis=0,
        )
        q_rows = dot(perm, q_rows.astype(BF16)).astype(BF16)
        fresh_k = new_rows[0, :, cols].astype(BF16)
        fresh_v = new_rows[1, :, cols].astype(BF16)
        scores = []
        for r in range(4):
            k_r = kbuf[16 * r : 16 * r + 16, :, cols].reshape(256, HEAD)
            score = dot_last(q_rows[64 * r : 64 * r + 64], k_r) * scale
            scores.append(jnp.where(position < lengths[r], score, LOW))
        scores = jnp.concatenate(scores, axis=0)
        fscores = jnp.where(fvisible, dot_last(q_rows, fresh_k) * scale, LOW)
        top = jnp.maximum(
            jnp.max(scores, axis=1, keepdims=True), jnp.max(fscores, axis=1, keepdims=True)
        )
        weights = jnp.exp(scores - top)
        fweights = jnp.exp(fscores - top)
        total = jnp.sum(weights, axis=1, keepdims=True) + jnp.sum(fweights, axis=1, keepdims=True)
        weights = weights.astype(BF16)
        accs = [
            dot(
                weights[64 * r : 64 * r + 64],
                vbuf[16 * r : 16 * r + 16, :, cols].reshape(256, HEAD),
            )
            for r in range(4)
        ]
        acc = jnp.concatenate(accs, axis=0) + dot(fweights.astype(BF16), fresh_v)
        acc = dot(perm_back, acc.astype(BF16)).astype(BF16)
        stats = jnp.zeros((256, HEAD), F32)
        for i, piece in enumerate(split_three(top) + split_three(total)):
            stats = jnp.where(stat_lane == i, piece, stats)
        stats = jnp.transpose(stats)[0:16].astype(BF16)
        stats = dot(stats, perm).astype(BF16)
        for q in range(4):
            part_send[k * 4 + q, 0:64] = acc[64 * q : 64 * q + 64]
            part_send[k * 4 + q, 64:80] = stats[:, 128 * (q >> 1) : 128 * (q >> 1) + 128]

    far = 1 - (t >> 2)
    attend(far)
    pl.semaphore_wait(barrier, DP - 1 + TP - 1)
    mine_at = t & 3
    for q in range(4):
        part_copy(lax.rem(far * 4 + q + TP - t, TP)).start()
    attend(1 - far)
    for q in range(1, 4):
        part_copy(lax.rem((1 - far) * 4 + ((mine_at + q) & 3) + TP - t, TP)).start()

    def wait_recv(ref, sem):
        pltpu.make_async_copy(ref, ref, sem).wait()

    pending = []

    def finish():
        for wait in pending:
            wait()
        pending.clear()

    def finish_parts():
        for d in range(1, TP):
            part_copy(d).wait_send()

    pending.append(finish_parts)
    part_recv[t] = part_send[t]

    dest = jnp.broadcast_to(page_dest[...], (64, 64))
    page_row = iota((64, 64), 0)
    page_col = iota((64, 64), 1)
    dest_of = jnp.sum(jnp.where(page_row == page_col, dest, 0), axis=1, keepdims=True)
    earlier = (dest == dest_of) & (page_col < page_row)
    within = jnp.sum(jnp.where(earlier, 1, 0), axis=1, keepdims=True)
    hit = dest_of * 4 + within == iota((64, 128), 1)
    number = iota((64, 128), 0) - 64
    inverse_row[...] = 64 + jnp.sum(jnp.where(hit, number, 0), axis=0, keepdims=True)
    to_scalars = local(inverse_row, inverse, 16)
    to_scalars.start()

    to_scalars.wait()

    @pl.loop(0, 128)
    def _(slot):
        page = jnp.clip(inverse[0, slot], 0, 64)
        ksend[slot] = kbuf[page]
        vsend[slot] = vbuf[page]

    def page_copy(which, d):
        dest = lax.rem(me + d, DP)
        src, dst = ((ksend, moved_keys), (vsend, moved_values))[which]
        return pltpu.make_async_remote_copy(
            src_ref=src.at[pl.ds(dest * 4, 4)],
            dst_ref=dst.at[pl.ds(me * 4, 4)],
            send_sem=page_send_sem.at[which],
            recv_sem=page_recv_sem.at[which],
            device_id=(dest, t),
            device_id_type=MESH,
        )

    def send_pages(first, last):
        @pl.loop(first, last)
        def _(d):
            page_copy(0, d).start()
            page_copy(1, d).start()

    send_pages(1, EARLY)

    own_k = local(ksend.at[pl.ds(me * 4, 4)], moved_keys.at[pl.ds(me * 4, 4)], 6)
    own_v = local(vsend.at[pl.ds(me * 4, 4)], moved_values.at[pl.ds(me * 4, 4)], 7)
    own_k.start()
    own_v.start()

    def finish_pages():
        own_k.wait()
        own_v.wait()

        others = pl.ds(0, 4 * (DP - 1))
        for which, ref in enumerate((moved_keys, moved_values)):
            wait_recv(ref.at[others], page_recv_sem.at[which])
            wait_recv(ref.at[others], page_send_sem.at[which])


    for d in range(1, TP):
        src = lax.rem(t + d, TP)
        wait_recv(part_recv.at[src], part_rsem.at[src])
    tops, sums = [], []
    for s in range(TP):
        stat = part_recv[s, 64:80].astype(F32)
        tops.append(stat[0:1] + stat[1:2] + stat[2:3])
        sums.append(stat[3:4] + stat[4:5] + stat[5:6])
    tops = jnp.concatenate(tops, axis=0)
    sums = jnp.concatenate(sums, axis=0)
    scales = jnp.exp(tops - jnp.max(tops, axis=0, keepdims=True))
    scales = scales / jnp.sum(scales * sums, axis=0, keepdims=True)
    scales = jnp.concatenate([scales, jnp.zeros((120, HEAD), F32)], axis=0)
    coeff[...] = jnp.transpose(scales)
    mine = coeff[pl.ds(pl.multiple_of((t & 1) * 64, 64), 64), :]
    merged = jnp.zeros((64, HEAD), F32)
    for s in range(TP):
        merged = merged + mine[:, s : s + 1] * part_recv[s, 0:64].astype(F32)
    merged = merged.astype(BF16)
    for h in range(4):
        attended[t, :, h * HEAD : (h + 1) * HEAD] = merged[h * 16 : h * 16 + 16]

    def att_copy(d):
        return pltpu.make_async_remote_copy(
            src_ref=attended.at[t],
            dst_ref=attended.at[t],
            send_sem=att_ssem.at[d],
            recv_sem=att_rsem.at[t],
            device_id=(me, lax.rem(t + d, TP)),
            device_id_type=MESH,
        )

    def send_att(d):
        att_copy(d).start()
        pending.append(lambda: att_copy(d).wait_send())

    for d in range(1, TP):
        send_att(d)

    named = rows_together(ids, idrows)
    prob = rows_together(probs, idrows)
    expert = iota((TOKENS, DP), 1).astype(F32)
    member = jnp.zeros((TOKENS, DP), F32)
    weight = jnp.zeros((TOKENS, DP), F32)
    for j in range(8):
        same = named[:, j : j + 1] == expert
        member = member + jnp.where(same, 1.0, 0.0)
        weight = weight + jnp.where(same, prob[:, j : j + 1], 0.0)
    member = member.astype(BF16)
    below = onehot(iota((TOKENS, TOKENS), 1) < iota((TOKENS, TOKENS), 0))
    rank = dot(below, member).astype(BF16)
    lane_expert = onehot((iota((DP, DP * BLOCK), 1) >> 4) == iota((DP, DP * BLOCK), 0))
    lane = iota((TOKENS, DP * BLOCK), 1)
    chosen = jnp.where(
        dot(rank, lane_expert) == (lane & 7).astype(F32), dot(member, lane_expert), 0.0
    )
    first = jnp.where((lane & 8) == 0, chosen, 0.0)
    scatter_back = jnp.concatenate([first, chosen - first], axis=0)
    scatter = jnp.transpose(scatter_back).astype(BF16)
    weight_top = weight.astype(BF16)
    weight_rest = (weight - weight_top.astype(F32)).astype(BF16)
    gather_top, gather_rest = [
        jnp.concatenate([part, part], axis=0) for part in (
            dot(weight_top, lane_expert), dot(weight_rest, lane_expert))
    ]
    gather_top = (gather_top * scatter_back).astype(BF16)
    gather_rest = (gather_rest * scatter_back).astype(BF16)

    prow = iota((ROWS, DP * BLOCK), 0)
    pcol = iota((ROWS, DP * BLOCK), 1)
    place = (prow & 31) * BLOCK + (prow >> 5)
    rrow = iota((DP * BLOCK, ROWS), 0)
    rcol = iota((DP * BLOCK, ROWS), 1)
    rplace = (rrow & 7) * DP + (rrow >> 4)
    for h in range(2):
        pick_in[h] = onehot(pcol == place + h * PAD_SLOTS)
        pick_out[h] = onehot((rcol == rplace) & (((rrow >> 3) & 1) == h))

    loads[2].wait()

    def project(src):
        return dot(attended[src], wo[pl.ds(pl.multiple_of(src * PART, PART), PART), :])

    projected = project(t)
    for d in (1, 7, 2, 6, 3, 5, 4):
        src = lax.rem(t + d, TP)
        wait_recv(attended.at[src], att_rsem.at[src])
        projected = projected + project(src)
    layer_state = (residual_rows + projected).astype(BF16)
    state[...] = layer_state

    stacked = jnp.concatenate([layer_state[:, :WIDE], layer_state[:, WIDE:]], axis=0)
    disp_send[...] = dot(scatter, stacked).astype(BF16)

    def block_of(ref, rank):
        return ref.at[pl.ds(pl.multiple_of(rank * BLOCK, BLOCK), BLOCK)]

    def all_copy(send, recv, ssem, rsem, d):
        dest = lax.rem(me + d, DP)
        return pltpu.make_async_remote_copy(
            src_ref=block_of(send, dest),
            dst_ref=block_of(recv, me),
            send_sem=ssem.at[0],
            recv_sem=rsem.at[0],
            device_id=(dest, t),
            device_id_type=MESH,
        )

    def exchange(send, recv, ssem, rsem):
        @pl.loop(1, DP)
        def _(d):
            all_copy(send, recv, ssem, rsem, d).start()

        block = pl.ds(pl.multiple_of(me * BLOCK, BLOCK), BLOCK)
        recv[block, :] = send[block, :]
        finish()
        others = pl.ds(0, BLOCK * (DP - 1))
        wait_recv(recv.at[others], rsem.at[0])
        pending.append(lambda: wait_recv(send.at[others], ssem.at[0]))

    exchange(disp_send, disp_recv, disp_ssem, disp_rsem)
    send_pages(EARLY, DP)
    pending.append(finish_pages)

    arrived = disp_recv[...]
    pieces = [dot(pick_in[h], arrived) for h in range(2)]
    for h in range(2):
        features = slice(h * WIDE, (h + 1) * WIDE)
        xbuf[t, :, features] = (pieces[h] * gain[:, features]).astype(BF16)
    toward = (lax.rem(t + 1, TP), lax.rem(t + TP - 1, TP))

    def rows_of(way, i):
        sub = i % SUBS
        return pl.ds((sub if way == 0 else SUBS - 1 - sub) * SUB_ROWS, SUB_ROWS)

    def ring_piece(way, i, step):
        chunk = lax.rem(t + (TP - step if way == 0 else step), TP)
        return xbuf.at[chunk, rows_of(way, i)]

    def ring_copy(way, i):
        piece = ring_piece(way, i, i // SUBS)
        return pltpu.make_async_remote_copy(
            src_ref=piece,
            dst_ref=piece,
            send_sem=ring_ssem.at[way, i],
            recv_sem=ring_rsem.at[way, i],
            device_id=(me, toward[way]),
            device_id_type=MESH,
        )

    def ring_wait(way, i):
        wait_recv(ring_piece(way, i, i // SUBS + 1), ring_rsem.at[way, i])

    def expert_in(chunk, first=False):
        x = xbuf[chunk]
        features = pl.ds(pl.multiple_of(chunk * PART, PART), PART)
        gate_part = dot_last(x, wg[:, features])
        up_part = dot_last(x, wu[:, features])
        if first:
            gate_acc[...] = gate_part
            up_acc[...] = up_part
        else:
            gate_acc[...] += gate_part
            up_acc[...] += up_part

    def send_ring(way, i):
        ring_copy(way, i).start()
        pending.append(lambda: ring_copy(way, i).wait_send())

    for i in range(SUBS):
        for way in range(2):
            send_ring(way, i)

    square = jnp.sum(pieces[0] * pieces[0], axis=1, keepdims=True)
    square = square + jnp.sum(pieces[1] * pieces[1], axis=1, keepdims=True)
    square = jnp.concatenate([square, jnp.zeros((256 - ROWS, 1), F32)], axis=0)
    sqbuf[t] = jnp.transpose(jnp.broadcast_to(square, (256, HEAD)))[0:1]

    def sq_copy(d):
        return pltpu.make_async_remote_copy(
            src_ref=sqbuf.at[t],
            dst_ref=sqbuf.at[t],
            send_sem=sq_ssem.at[d],
            recv_sem=sq_rsem.at[t],
            device_id=(me, lax.rem(t + d, TP)),
            device_id_type=MESH,
        )

    def send_sq(d):
        sq_copy(d).start()
        pending.append(lambda: sq_copy(d).wait_send())

    for d in range(1, TP):
        send_sq(d)

    loads[3].wait()
    loads[4].wait()
    expert_in(t, first=True)
    for i in range(MESSAGES):
        for way in range(2):
            ring_wait(way, i)
            if i + SUBS < MESSAGES:
                send_ring(way, i + SUBS)
        if i % SUBS == SUBS - 1:
            expert_in(lax.rem(t + TP - (i // SUBS + 1), TP))
            expert_in(lax.rem(t + i // SUBS + 1, TP))
    expert_in(lax.rem(t + 4, TP))

    for d in range(1, TP):
        src = lax.rem(t + d, TP)
        wait_recv(sqbuf.at[src], sq_rsem.at[src])
    total = sqbuf[0]
    for s in range(1, TP):
        total = total + sqbuf[s]
    inv_norm = lax.rsqrt(total * (1.0 / (TP * PART)) + EPSILON)
    inv_norm = jnp.transpose(jnp.broadcast_to(inv_norm, (HEAD, 256)))[0:ROWS, 0:1]
    gate_part = gate_acc[...] * inv_norm
    up_part = up_acc[...] * inv_norm
    hidden = (gate_part / (1.0 + jnp.exp(-gate_part)) * up_part).astype(BF16)

    loads[5].wait()
    sends = (rsend, lsend)
    recvs = (rrecv, lrecv)

    def expert_out(chunk):
        ybuf[chunk] = dot(hidden, wd[:, pl.ds(pl.multiple_of(chunk * PART, PART), PART)])

    def red_copy(way, j):
        return pltpu.make_async_remote_copy(
            src_ref=sends[way].at[j],
            dst_ref=recvs[way].at[j],
            send_sem=red_ssem.at[way, j],
            recv_sem=red_rsem.at[way, j],
            device_id=(me, toward[way]),
            device_id_type=MESH,
        )

    def send_red(way, j):
        red_copy(way, j).start()
        pending.append(lambda: red_copy(way, j).wait_send())

    for j in range(MESSAGES):
        step = (j + SUBS // 2) // SUBS
        sub_at = (j + SUBS // 2) % SUBS
        for way in range(2):
            distance = 4 - step
            chunk = lax.rem(t + (distance if way == 0 else TP - distance), TP)
            if sub_at == 0 or (j == 0 and way == 0):
                expert_out(chunk)
            sub = sub_at if way == 0 else SUBS - 1 - sub_at
            value = ybuf[chunk, sub * SUB_ROWS : (sub + 1) * SUB_ROWS]
            if j >= SUBS:
                wait_recv(recvs[way].at[j - SUBS], red_rsem.at[way, j - SUBS])
                value = value + recvs[way][j - SUBS].astype(F32)
            sends[way][j] = value.astype(BF16)
            send_red(way, j)
    expert_out(t)
    for j in range(MESSAGES - SUBS, MESSAGES):
        for way in range(2):
            wait_recv(recvs[way].at[j], red_rsem.at[way, j])
    results = []
    for sub in range(SUBS):
        value = ybuf[t, sub * SUB_ROWS : (sub + 1) * SUB_ROWS]
        value = value + recvs[0][MESSAGES - SUBS + sub].astype(F32)
        value = value + recvs[1][MESSAGES - 1 - sub].astype(F32)
        results.append(value.astype(BF16))
    result = jnp.concatenate(results, axis=0)

    back = dot(pick_out[0], result[:, :WIDE]) + dot(pick_out[1], result[:, WIDE:])
    ret_send[...] = back.astype(BF16)
    exchange(ret_send, ret_recv, ret_ssem, ret_rsem)

    returned = ret_recv[...]
    mixture = dot(gather_top, returned) + dot(gather_rest, returned)
    for h in range(2):
        features = slice(h * WIDE, (h + 1) * WIDE)
        total = state[:, features].astype(F32) + mixture[h * TOKENS : (h + 1) * TOKENS]
        for r in range(4):
            layer_out[r, :, features] = total[4 * r : 4 * r + 4].astype(BF16)

    finish()


def layer(*operands):
    smem = pl.BlockSpec(memory_space=pltpu.SMEM)
    vmem = pl.BlockSpec(memory_space=pltpu.VMEM)
    hbm = pl.BlockSpec(memory_space=pltpu.HBM)
    anywhere = pl.BlockSpec(memory_space=pl.ANY)
    dma = pltpu.SemaphoreType.DMA
    return pl.pallas_call(
        layer_kernel,
        out_shape=(
            jax.ShapeDtypeStruct((128, 16, WIDE), BF16),
            jax.ShapeDtypeStruct((128, 16, WIDE), BF16),
            jax.ShapeDtypeStruct((4, 4, PART), BF16),
        ),
        in_specs=[smem] + [hbm] * 14,
        out_specs=(anywhere, anywhere, vmem),
        scratch_shapes=[
            pltpu.VMEM((1, 64), jnp.int32),
            pltpu.VMEM((4, 4, 4096), BF16),
            pltpu.VMEM((4, 4, WIDE), BF16),
            pltpu.VMEM((4, 4, WIDE), BF16),
            pltpu.VMEM((4, 4, PART), BF16),
            pltpu.VMEM((1, PART), F32),
            pltpu.VMEM((4, 4, 8), jnp.int32),
            pltpu.VMEM((4, 4, 8), F32),
            pltpu.VMEM((TOKENS, 4096), F32),
            pltpu.VMEM((TOKENS, PART), F32),
            pltpu.VMEM((2, TOKENS, WIDE), F32),
            pltpu.VMEM((1, 128), jnp.int32),
            pltpu.SMEM((1, 128), jnp.int32),
            pltpu.VMEM((2, ROWS, DP * BLOCK), BF16),
            pltpu.VMEM((2, DP * BLOCK, ROWS), BF16),
            pltpu.VMEM((65, 16, WIDE), BF16),
            pltpu.VMEM((65, 16, WIDE), BF16),
            pltpu.VMEM((128, 16, WIDE), BF16),
            pltpu.VMEM((128, 16, WIDE), BF16),
            pltpu.VMEM((4096, PART), BF16),
            pltpu.VMEM((192, 4096), BF16),
            pltpu.VMEM((192, 4096), BF16),
            pltpu.VMEM((192, 4096), BF16),
            pltpu.VMEM((TP, 80, HEAD), BF16),
            pltpu.VMEM((TP, 80, HEAD), BF16),
            pltpu.VMEM((HEAD, HEAD), F32),
            pltpu.VMEM((TP, TOKENS, PART), BF16),
            pltpu.VMEM((TOKENS, PART), BF16),
            pltpu.VMEM((DP * BLOCK, WIDE), BF16),
            pltpu.VMEM((DP * BLOCK, WIDE), BF16),
            pltpu.VMEM((TP, ROWS, PART), BF16),
            pltpu.VMEM((TP, 1, 256), F32),
            pltpu.VMEM((ROWS, 192), F32),
            pltpu.VMEM((ROWS, 192), F32),
            pltpu.VMEM((TP, ROWS, PART), F32),
            pltpu.VMEM((MESSAGES, SUB_ROWS, PART), BF16),
            pltpu.VMEM((MESSAGES, SUB_ROWS, PART), BF16),
            pltpu.VMEM((MESSAGES, SUB_ROWS, PART), BF16),
            pltpu.VMEM((MESSAGES, SUB_ROWS, PART), BF16),
            pltpu.VMEM((DP * BLOCK, WIDE), BF16),
            pltpu.VMEM((DP * BLOCK, WIDE), BF16),
            dma((17,)),
            dma((2,)), dma((2,)),
            dma((TP,)), dma((TP,)), dma((TP,)), dma((TP,)),
            dma((1,)), dma((1,)),
            dma((TP,)), dma((TP,)),
            dma((2, MESSAGES)), dma((2, MESSAGES)), dma((2, MESSAGES)), dma((2, MESSAGES)),
            dma((1,)), dma((1,)),
        ],
        compiler_params=pltpu.CompilerParams(
            collective_id=0, has_side_effects=True, vmem_limit_bytes=60 * 1024 * 1024
        ),
    )(*operands)


def place_kernel(keys, values, rows, keys_out, values_out, rows_out, kbuf, vbuf, rbuf, sems):
    moves = [(rows, rbuf, rows_out)]
    for i in range(4):
        for src, buf, dst in ((keys, kbuf, keys_out), (values, vbuf, values_out)):
            part = pl.ds(i * 32, 32)
            moves.append((src.at[part], buf.at[part], dst.at[part]))
    loads = [
        pltpu.make_async_copy(src, buf, sems.at[0, i]) for i, (src, buf, _) in enumerate(moves)
    ]
    stores = [
        pltpu.make_async_copy(buf, dst, sems.at[1, i]) for i, (_, buf, dst) in enumerate(moves)
    ]
    for load in loads:
        load.start()
    for load, store in zip(loads, stores):
        load.wait()
        store.start()
    for store in stores:
        store.wait()


def place(*arrays):
    hbm = pl.BlockSpec(memory_space=pltpu.HBM)
    return pl.pallas_call(
        place_kernel,
        out_shape=tuple(jax.ShapeDtypeStruct(a.shape, a.dtype) for a in arrays),
        in_specs=[pl.BlockSpec(memory_space=pl.ANY)] * 3,
        out_specs=(hbm,) * 3,
        scratch_shapes=[pltpu.VMEM(a.shape, a.dtype) for a in arrays]
        + [pltpu.SemaphoreType.DMA((2, 9))],
        compiler_params=pltpu.CompilerParams(vmem_limit_bytes=60 * 1024 * 1024),
    )(*arrays)


def shards(
    cache_keys, cache_values, page_dest, lengths, queries, new_keys, new_values, residual,
    out_weight, norm_gain, expert_ids, gate_probs, w_gate, w_up, w_down,
):
    return place(*layer(
        lengths,
        page_dest.reshape(1, -1),
        queries,
        new_keys,
        new_values,
        residual,
        norm_gain[None, :],
        expert_ids,
        gate_probs,
        cache_keys,
        cache_values,
        out_weight,
        w_gate[0].T,
        w_up[0].T,
        w_down[0],
    ))


def solution(mesh):
    in_specs = (
        P("dp", "tp", None),
        P("dp", "tp", None),
        P("dp", None),
        P("dp"),
        P("dp", None, None),
        P("dp", None, None),
        P("dp", None, None),
        P("dp", None, "tp"),
        P(None, "tp"),
        P("tp"),
        P("dp", None, None),
        P("dp", None, None),
        P("dp", None, "tp"),
        P("dp", None, "tp"),
        P("dp", "tp", None),
    )
    out_specs = (P("dp", "tp", None), P("dp", "tp", None), P("dp", None, "tp"))
    return jax.shard_map(shards, mesh=mesh, in_specs=in_specs, out_specs=out_specs, check_vma=False)
```

```python
import math

import jax
import jax.numpy as jnp
from jax import lax
from jax.experimental import pallas as pl
from jax.experimental.pallas import tpu as pltpu
from jax.sharding import PartitionSpec as P

MESH = pl.DeviceIdType.MESH
F32 = jnp.float32
BF16 = jnp.bfloat16

DP = 32
TP = 8
HEAD = 128
TOKENS = 16
SLOTS = 6
PAD_SLOTS = 8
ROWS = DP * SLOTS
BLOCK = 16
GROUP = 8
GROUP_ROWS = GROUP * BLOCK
PART = 512
WIDE = 256
EPSILON = 1e-06
LOW = -1e30
ARRIVAL = (0, 1, 3, 2)
RETURN_ORDER = (2, 1, 3, 0)
RING = 3
FAR = (4,)
EARLY = 12
MIDDLE = 6
PAGES_A_STEP = 2
SUBS = 4
SUB_ROWS = ROWS // SUBS
MESSAGES = RING * SUBS


def iota(shape, dim):
    return lax.broadcasted_iota(jnp.int32, shape, dim)


def onehot(mask):
    return jnp.where(mask, 1.0, 0.0).astype(BF16)


def dot(a, b):
    return jnp.dot(a, b, preferred_element_type=F32)


def dot_last(a, b):
    return lax.dot_general(a, b, (((1,), (1,)), ((), ())), preferred_element_type=F32)


def split_three(value):
    top = value.astype(BF16).astype(F32)
    rest = value - top
    middle = rest.astype(BF16).astype(F32)
    return top, middle, rest - middle


def layer_kernel(
    lengths, page_dest_in, queries_in, new_keys_in, new_values_in, residual_in, gain_in, ids_in,
    probs_in, keys, values, out_weight, w_gate, w_up, w_down,
    moved_keys, moved_values, layer_out,
    page_dest, queries, new_keys, new_values, residual, gain, ids, probs,
    qrows, idrows, new_rows, inverse_row, inverse, pick_in, pick_out, xwide,
    far_send, far_recv, fdisp_send, fdisp_recv, fret_send, fret_recv, mix_send, mix_recv,
    kbuf, vbuf, ksend, vsend, wo, wg, wu, wd,
    part_send, part_recv, coeff, attended, state,
    disp_send, disp_recv, xbuf, sqbuf, gate_acc, up_acc, ybuf,
    lsend, rsend, lrecv, rrecv, ret_send, ret_recv,
    local_sem, page_send_sem, page_recv_sem, part_ssem, part_rsem, att_ssem, att_rsem,
    disp_ssem, disp_rsem, sq_ssem, sq_rsem, ring_ssem, ring_rsem, red_ssem, red_rsem,
    ret_ssem, ret_rsem,
    far_ssem, far_rsem, fdisp_ssem, fdisp_rsem, fret_ssem, fret_rsem, mix_ssem, mix_rsem,
):
    me = lax.axis_index("dp")
    t = lax.axis_index("tp")

    def local(src, dst, i):
        return pltpu.make_async_copy(src, dst, local_sem.at[i])

    small = [
        local(src, dst, 8 + i)
        for i, (src, dst) in enumerate((
            (page_dest_in, page_dest), (queries_in, queries), (new_keys_in, new_keys),
            (new_values_in, new_values), (residual_in, residual), (gain_in, gain),
            (ids_in, ids), (probs_in, probs),
        ))
    ]
    loads = [
        local(keys, kbuf.at[pl.ds(0, 64)], 0),
        local(values, vbuf.at[pl.ds(0, 64)], 1),
        local(out_weight, wo, 2),
        local(w_gate, wg, 3),
        local(w_up, wu, 4),
        local(w_down, wd, 5),
    ]
    for load in small + loads[:2]:
        load.start()

    barrier = pltpu.get_barrier_semaphore()

    @pl.loop(1, DP)
    def _(d):
        pl.semaphore_signal(
            barrier, inc=1, device_id=(lax.rem(me + d, DP), t), device_id_type=MESH
        )

    for d in range(1, TP):
        pl.semaphore_signal(
            barrier, inc=1, device_id=(me, lax.rem(t + d, TP)), device_id_type=MESH
        )

    kbuf[64] = jnp.zeros((16, WIDE), BF16)
    vbuf[64] = jnp.zeros((16, WIDE), BF16)
    for load in small:
        load.wait()

    def rows_together(ref, scratch):
        for r in range(4):
            scratch[4 * r : 4 * r + 4, : ref.shape[2]] = ref[r].astype(F32)
        return scratch[:, : ref.shape[2]]

    rows_together(new_keys, new_rows.at[0])
    rows_together(new_values, new_rows.at[1])
    residual_rows = rows_together(residual, idrows)
    rows_together(queries, qrows)

    loads[0].wait()
    loads[1].wait()
    for load in loads[2:]:
        load.start()

    row = iota((256, 256), 0)
    col = iota((256, 256), 1)
    perm = onehot(col == ((row >> 2) & 15) * 16 + (row >> 6) * 4 + (row & 3))
    perm_back = onehot(col == ((row >> 2) & 3) * 64 + (row >> 4) * 4 + (row & 3))
    scale = 1.0 / math.sqrt(HEAD)
    lane = iota((64, 256), 1)
    position = (lane >> 4) * 128 + t * 16 + (lane & 15)
    frow = iota((256, TOKENS), 0)
    fcol = iota((256, TOKENS), 1)
    fvisible = ((fcol >> 2) == (frow >> 6)) & ((fcol & 3) <= (frow & 3)) & (t == 0)
    stat_lane = iota((256, HEAD), 1)

    def part_copy(d):
        dest = lax.rem(t + d, TP)
        return pltpu.make_async_remote_copy(
            src_ref=part_send.at[dest],
            dst_ref=part_recv.at[t],
            send_sem=part_ssem.at[d],
            recv_sem=part_rsem.at[t],
            device_id=(me, dest),
            device_id_type=MESH,
        )

    def attend(k):
        cols = pl.ds(pl.multiple_of(k * HEAD, HEAD), HEAD)
        q_rows = jnp.concatenate(
            [
                qrows[:, pl.ds(pl.multiple_of((k * 16 + g) * HEAD, HEAD), HEAD)]
                for g in range(16)
            ],
            axis=0,
        )
        q_rows = dot(perm, q_rows.astype(BF16)).astype(BF16)
        fresh_k = new_rows[0, :, cols].astype(BF16)
        fresh_v = new_rows[1, :, cols].astype(BF16)
        scores = []
        for r in range(4):
            k_r = kbuf[16 * r : 16 * r + 16, :, cols].reshape(256, HEAD)
            score = dot_last(q_rows[64 * r : 64 * r + 64], k_r) * scale
            scores.append(jnp.where(position < lengths[r], score, LOW))
        scores = jnp.concatenate(scores, axis=0)
        fscores = jnp.where(fvisible, dot_last(q_rows, fresh_k) * scale, LOW)
        top = jnp.maximum(
            jnp.max(scores, axis=1, keepdims=True), jnp.max(fscores, axis=1, keepdims=True)
        )
        weights = jnp.exp(scores - top)
        fweights = jnp.exp(fscores - top)
        total = jnp.sum(weights, axis=1, keepdims=True) + jnp.sum(fweights, axis=1, keepdims=True)
        weights = weights.astype(BF16)
        accs = [
            dot(
                weights[64 * r : 64 * r + 64],
                vbuf[16 * r : 16 * r + 16, :, cols].reshape(256, HEAD),
            )
            for r in range(4)
        ]
        acc = jnp.concatenate(accs, axis=0) + dot(fweights.astype(BF16), fresh_v)
        acc = dot(perm_back, acc.astype(BF16)).astype(BF16)
        stats = jnp.zeros((256, HEAD), F32)
        for i, piece in enumerate(split_three(top) + split_three(total)):
            stats = jnp.where(stat_lane == i, piece, stats)
        stats = jnp.transpose(stats)[0:16].astype(BF16)
        stats = dot(stats, perm).astype(BF16)
        for q in range(4):
            part_send[k * 4 + q, 0:64] = acc[64 * q : 64 * q + 64]
            part_send[k * 4 + q, 64:80] = stats[:, 128 * (q >> 1) : 128 * (q >> 1) + 128]

    far = 1 - (t >> 2)
    attend(far)
    pl.semaphore_wait(barrier, DP - 1 + TP - 1)
    mine_at = t & 3
    for q in range(4):
        part_copy(lax.rem(far * 4 + q + TP - t, TP)).start()
    attend(1 - far)
    for q in range(1, 4):
        part_copy(lax.rem((1 - far) * 4 + ((mine_at + q) & 3) + TP - t, TP)).start()

    def wait_recv(ref, sem):
        pltpu.make_async_copy(ref, ref, sem).wait()

    pending = []

    def finish():
        for wait in pending:
            wait()
        pending.clear()

    def finish_parts():
        for d in range(1, TP):
            part_copy(d).wait_send()

    pending.append(finish_parts)
    part_recv[t] = part_send[t]

    dest = jnp.broadcast_to(page_dest[...], (64, 64))
    page_row = iota((64, 64), 0)
    page_col = iota((64, 64), 1)
    dest_of = jnp.sum(jnp.where(page_row == page_col, dest, 0), axis=1, keepdims=True)
    earlier = (dest == dest_of) & (page_col < page_row)
    within = jnp.sum(jnp.where(earlier, 1, 0), axis=1, keepdims=True)
    hit = dest_of * 4 + within == iota((64, 128), 1)
    number = iota((64, 128), 0) - 64
    inverse_row[...] = 64 + jnp.sum(jnp.where(hit, number, 0), axis=0, keepdims=True)
    to_scalars = local(inverse_row, inverse, 16)
    to_scalars.start()

    to_scalars.wait()

    @pl.loop(0, 128)
    def _(slot):
        page = jnp.clip(inverse[0, slot], 0, 64)
        ksend[slot] = kbuf[page]
        vsend[slot] = vbuf[page]

    begin = 11 * (me & 1) + 5 * ((me >> 1) & 3) + 8 * (me >> 3)

    def page_copy(which, d):
        dest = lax.rem(me + 1 + lax.rem(d + begin, DP - 1), DP)
        src, dst = ((ksend, moved_keys), (vsend, moved_values))[which]
        return pltpu.make_async_remote_copy(
            src_ref=src.at[pl.ds(dest * 4, 4)],
            dst_ref=dst.at[pl.ds(me * 4, 4)],
            send_sem=page_send_sem.at[which],
            recv_sem=page_recv_sem.at[which],
            device_id=(dest, t),
            device_id_type=MESH,
        )

    own_k = local(ksend.at[pl.ds(me * 4, 4)], moved_keys.at[pl.ds(me * 4, 4)], 6)
    own_v = local(vsend.at[pl.ds(me * 4, 4)], moved_values.at[pl.ds(me * 4, 4)], 7)
    def finish_pages():
        own_k.wait()
        own_v.wait()

        others = pl.ds(0, 4 * (DP - 1))
        for which, ref in enumerate((moved_keys, moved_values)):
            wait_recv(ref.at[others], page_recv_sem.at[which])
            wait_recv(ref.at[others], page_send_sem.at[which])

    def send_pages(first, last):
        @pl.loop(first, last)
        def _(d):
            page_copy(0, d).start()
            page_copy(1, d).start()

    own_k.start()
    own_v.start()
    send_pages(1, 1 + EARLY)

    for d in range(1, TP):
        src = lax.rem(t + d, TP)
        wait_recv(part_recv.at[src], part_rsem.at[src])
    tops, sums = [], []
    for s in range(TP):
        stat = part_recv[s, 64:80].astype(F32)
        tops.append(stat[0:1] + stat[1:2] + stat[2:3])
        sums.append(stat[3:4] + stat[4:5] + stat[5:6])
    tops = jnp.concatenate(tops, axis=0)
    sums = jnp.concatenate(sums, axis=0)
    scales = jnp.exp(tops - jnp.max(tops, axis=0, keepdims=True))
    scales = scales / jnp.sum(scales * sums, axis=0, keepdims=True)
    scales = jnp.concatenate([scales, jnp.zeros((120, HEAD), F32)], axis=0)
    coeff[...] = jnp.transpose(scales)
    mine = coeff[pl.ds(pl.multiple_of((t & 1) * 64, 64), 64), :]
    merged = jnp.zeros((64, HEAD), F32)
    for s in range(TP):
        merged = merged + mine[:, s : s + 1] * part_recv[s, 0:64].astype(F32)
    merged = merged.astype(BF16)
    for h in range(4):
        attended[t, :, h * HEAD : (h + 1) * HEAD] = merged[h * 16 : h * 16 + 16]

    def att_copy(d):
        return pltpu.make_async_remote_copy(
            src_ref=attended.at[t],
            dst_ref=attended.at[t],
            send_sem=att_ssem.at[d],
            recv_sem=att_rsem.at[t],
            device_id=(me, lax.rem(t + d, TP)),
            device_id_type=MESH,
        )

    def send_att(d):
        att_copy(d).start()
        pending.append(lambda: att_copy(d).wait_send())

    for d in (4, 3, 5, 2, 6, 1, 7):
        send_att(d)

    named = rows_together(ids, idrows)
    prob = rows_together(probs, idrows)
    expert = iota((TOKENS, DP), 1).astype(F32)
    member = jnp.zeros((TOKENS, DP), F32)
    weight = jnp.zeros((TOKENS, DP), F32)
    for j in range(8):
        same = named[:, j : j + 1] == expert
        member = member + jnp.where(same, 1.0, 0.0)
        weight = weight + jnp.where(same, prob[:, j : j + 1], 0.0)
    member = member.astype(BF16)
    below = onehot(iota((TOKENS, TOKENS), 1) < iota((TOKENS, TOKENS), 0))
    rank = dot(below, member).astype(BF16)
    lane_expert = onehot((iota((DP, DP * BLOCK), 1) >> 4) == iota((DP, DP * BLOCK), 0))
    lane = iota((TOKENS, DP * BLOCK), 1)
    chosen = jnp.where(
        dot(rank, lane_expert) == (lane & 7).astype(F32), dot(member, lane_expert), 0.0
    )
    first = jnp.where((lane & 8) == 0, chosen, 0.0)
    scatter_back = jnp.concatenate([first, chosen - first], axis=0)
    scatter = jnp.transpose(scatter_back).astype(BF16)
    weight_top = weight.astype(BF16)
    weight_rest = (weight - weight_top.astype(F32)).astype(BF16)
    gather_top, gather_rest = [
        jnp.concatenate([part, part], axis=0) for part in (
            dot(weight_top, lane_expert), dot(weight_rest, lane_expert))
    ]
    gather_top = (gather_top * scatter_back).astype(BF16)
    gather_rest = (gather_rest * scatter_back).astype(BF16)

    prow = iota((SUB_ROWS, GROUP_ROWS), 0)
    pcol = iota((SUB_ROWS, GROUP_ROWS), 1)
    source = (prow * 683) >> 12
    place = source * BLOCK + prow - source * SLOTS
    rrow = iota((GROUP_ROWS, SUB_ROWS), 0)
    rcol = iota((GROUP_ROWS, SUB_ROWS), 1)
    rslot = rrow & 7
    rplace = (rrow >> 4) * SLOTS + rslot
    for h in range(2):
        pick_in[h] = onehot(pcol == place + h * PAD_SLOTS)
        pick_out[h] = onehot((rcol == rplace) & (rslot < SLOTS) & (((rrow >> 3) & 1) == h))

    loads[2].wait()

    def project(src):
        return dot(attended[src], wo[pl.ds(pl.multiple_of(src * PART, PART), PART), :])

    projected = project(t)
    for d in (1, 7, 2, 6, 3, 5, 4):
        src = lax.rem(t + d, TP)
        wait_recv(attended.at[src], att_rsem.at[src])
        projected = projected + project(src)
    layer_state = (residual_rows + projected).astype(BF16)
    state[...] = layer_state

    stacked = jnp.concatenate([layer_state[:, :WIDE], layer_state[:, WIDE:]], axis=0)
    disp_send[...] = dot(scatter, stacked).astype(BF16)

    def block_of(ref, rank):
        return ref.at[pl.ds(pl.multiple_of(rank * BLOCK, BLOCK), BLOCK)]

    group = me >> 3

    def group_at(offset):
        return (group + offset) & 3

    def blocks_of(ref, count):
        return ref.at[pl.ds(0, count * BLOCK)]

    def send_group(send, recv, ssem, rsem, offset):
        for i in range(1 if offset == 0 else 0, GROUP):
            dest = group_at(offset) * GROUP + ((me + i) & 7)
            pltpu.make_async_remote_copy(
                src_ref=block_of(send, dest),
                dst_ref=block_of(recv, me),
                send_sem=ssem.at[0],
                recv_sem=rsem,
                device_id=(dest, t),
                device_id_type=MESH,
            ).start()

    def keep_own(send, recv):
        block = pl.ds(pl.multiple_of(me * BLOCK, BLOCK), BLOCK)
        recv[block, :] = send[block, :]

    for offset in ARRIVAL:
        send_group(disp_send, disp_recv, disp_ssem, disp_rsem.at[group], offset)
    pending.append(lambda: wait_recv(blocks_of(disp_send, DP - 1), disp_ssem.at[0]))
    keep_own(disp_send, disp_recv)

    def far_copy(send, recv, ssem, rsem, f, dest):
        return pltpu.make_async_remote_copy(
            src_ref=send,
            dst_ref=recv.at[f],
            send_sem=ssem.at[f],
            recv_sem=rsem.at[f],
            device_id=(me, dest),
            device_id_type=MESH,
        )

    far_send[...] = (layer_state.astype(F32) * gain[...]).astype(BF16)

    def start_far(f):
        copy = far_copy(
            far_send, far_recv, far_ssem, far_rsem, f, lax.rem(t + FAR[f], TP)
        )
        copy.start()
        pending.append(copy.wait_send)

    for f in range(len(FAR)):
        start_far(f)

    def far_chunk(f):
        return lax.rem(t + TP - FAR[f], TP)

    chores = []

    def spread(send, recv, ssem, rsem, f):
        for offset in ARRIVAL:
            chores.append(
                lambda offset=offset: send_group(
                    send.at[f], recv.at[f], ssem.at[pl.ds(f, 1)], rsem.at[f], offset
                )
            )
        chores.append(lambda: keep_own(send.at[f], recv.at[f]))

    def pass_on(f):
        def scatter_far():
            wait_recv(far_recv.at[f], far_rsem.at[f])
            rows = far_recv[f]
            rows = jnp.concatenate([rows[:, :WIDE], rows[:, WIDE:]], axis=0)
            fdisp_send[f] = dot(scatter, rows).astype(BF16)

        chores.append(scatter_far)
        spread(fdisp_send, fdisp_recv, fdisp_ssem, fdisp_rsem, f)
        later.append(lambda: wait_recv(blocks_of(fdisp_send.at[f], DP - 1), fdisp_ssem.at[f]))

    later = []
    for f in range(len(FAR)):
        pass_on(f)
    page_chores = []
    for first in range(1 + EARLY, 1 + EARLY + MIDDLE, PAGES_A_STEP):
        page_chores.append(lambda first=first: send_pages(first, first + PAGES_A_STEP))
    chores.extend(page_chores)

    def chore():
        if chores:
            chores.pop(0)()

    def rows_at(offset):
        return pl.ds(pl.multiple_of(group_at(offset) * SUB_ROWS, SUB_ROWS), SUB_ROWS)

    toward = (lax.rem(t + 1, TP), lax.rem(t + TP - 1, TP))

    def ring_piece(way, i, step):
        chunk = lax.rem(t + (TP - step if way == 0 else step), TP)
        return xbuf.at[chunk, rows_at(ARRIVAL[i % SUBS])]

    def ring_copy(way, i):
        piece = ring_piece(way, i, i // SUBS)
        return pltpu.make_async_remote_copy(
            src_ref=piece,
            dst_ref=piece,
            send_sem=ring_ssem.at[way, i],
            recv_sem=ring_rsem.at[way, i],
            device_id=(me, toward[way]),
            device_id_type=MESH,
        )

    def ring_wait(way, i):
        wait_recv(ring_piece(way, i, i // SUBS + 1), ring_rsem.at[way, i])

    def expert_in(chunk, first=False):
        x = xbuf[chunk]
        features = pl.ds(pl.multiple_of(chunk * PART, PART), PART)
        gate_part = dot_last(x, wg[:, features])
        up_part = dot_last(x, wu[:, features])
        if first:
            gate_acc[...] = gate_part
            up_acc[...] = up_part
        else:
            gate_acc[...] += gate_part
            up_acc[...] += up_part

    def send_ring(way, i):
        ring_copy(way, i).start()
        pending.append(lambda: ring_copy(way, i).wait_send())

    for at, offset in enumerate(ARRIVAL):
        count = GROUP - 1 if offset == 0 else GROUP
        wait_recv(blocks_of(disp_recv, count), disp_rsem.at[group_at(offset)])
        arrived = disp_recv[
            pl.ds(pl.multiple_of(group_at(offset) * GROUP_ROWS, GROUP_ROWS), GROUP_ROWS), :
        ]
        for h in range(2):
            features = slice(h * WIDE, (h + 1) * WIDE)
            piece = dot(pick_in[h], arrived)
            xwide[rows_at(offset), features] = piece
            xbuf[t, rows_at(offset), features] = (piece * gain[:, features]).astype(BF16)
        for way in range(2):
            send_ring(way, at)

    square = jnp.sum(xwide[...] * xwide[...], axis=1, keepdims=True)
    square = jnp.concatenate([square, jnp.zeros((256 - ROWS, 1), F32)], axis=0)
    sqbuf[t] = jnp.transpose(jnp.broadcast_to(square, (256, HEAD)))[0:1]

    def sq_copy(d):
        return pltpu.make_async_remote_copy(
            src_ref=sqbuf.at[t],
            dst_ref=sqbuf.at[t],
            send_sem=sq_ssem.at[d],
            recv_sem=sq_rsem.at[t],
            device_id=(me, lax.rem(t + d, TP)),
            device_id_type=MESH,
        )

    def send_sq(d):
        sq_copy(d).start()
        pending.append(lambda: sq_copy(d).wait_send())

    for d in range(1, TP):
        send_sq(d)

    loads[3].wait()
    loads[4].wait()
    expert_in(t, first=True)
    for i in range(MESSAGES):
        for way in range(2):
            ring_wait(way, i)
            if i + SUBS < MESSAGES:
                send_ring(way, i + SUBS)
        chore()
        if i % SUBS == SUBS - 1:
            expert_in(lax.rem(t + TP - (i // SUBS + 1), TP))
            expert_in(lax.rem(t + i // SUBS + 1, TP))
    while len(chores) > len(page_chores):
        chore()
    for f in range(len(FAR)):
        wait_recv(blocks_of(fdisp_recv.at[f], DP - 1), fdisp_rsem.at[f])
        for g in range(4):
            arrived = fdisp_recv[f, g * GROUP_ROWS : (g + 1) * GROUP_ROWS]
            for h in range(2):
                xbuf[
                    far_chunk(f), g * SUB_ROWS : (g + 1) * SUB_ROWS, h * WIDE : (h + 1) * WIDE
                ] = dot(pick_in[h], arrived).astype(BF16)
        expert_in(far_chunk(f))

    for d in range(1, TP):
        src = lax.rem(t + d, TP)
        wait_recv(sqbuf.at[src], sq_rsem.at[src])
    total = sqbuf[0]
    for s in range(1, TP):
        total = total + sqbuf[s]
    inv_norm = lax.rsqrt(total * (1.0 / (TP * PART)) + EPSILON)
    inv_norm = jnp.transpose(jnp.broadcast_to(inv_norm, (HEAD, 256)))[0:ROWS, 0:1]
    gate_part = gate_acc[...] * inv_norm
    up_part = up_acc[...] * inv_norm
    hidden = (gate_part / (1.0 + jnp.exp(-gate_part)) * up_part).astype(BF16)

    loads[5].wait()
    sends = (rsend, lsend)
    recvs = (rrecv, lrecv)

    def expert_out(chunk):
        ybuf[chunk] = dot(hidden, wd[:, pl.ds(pl.multiple_of(chunk * PART, PART), PART)])

    def red_copy(way, j):
        return pltpu.make_async_remote_copy(
            src_ref=sends[way].at[j],
            dst_ref=recvs[way].at[j],
            send_sem=red_ssem.at[way, j],
            recv_sem=red_rsem.at[way, j],
            device_id=(me, toward[way]),
            device_id_type=MESH,
        )

    def send_red(way, j):
        red_copy(way, j).start()
        pending.append(lambda: red_copy(way, j).wait_send())

    def give_back(f):
        def group_back(offset):
            if offset == ARRIVAL[0]:
                expert_out(far_chunk(f))
            value = ybuf[far_chunk(f), rows_at(offset), :].astype(BF16)
            back = dot(pick_out[0], value[:, :WIDE]) + dot(pick_out[1], value[:, WIDE:])
            rows = pl.ds(pl.multiple_of(group_at(offset) * GROUP_ROWS, GROUP_ROWS), GROUP_ROWS)
            fret_send[f, rows, :] = back.astype(BF16)
            send_group(
                fret_send.at[f], fret_recv.at[f], fret_ssem.at[pl.ds(f, 1)], fret_rsem.at[f], offset
            )

        def mix_far():
            wait_recv(blocks_of(fret_recv.at[f], DP - 1), fret_rsem.at[f])
            returned = fret_recv[f]
            mixture = dot(gather_top, returned) + dot(gather_rest, returned)
            for h in range(2):
                mix_send[f, :, h * WIDE : (h + 1) * WIDE] = mixture[
                    h * TOKENS : (h + 1) * TOKENS
                ].astype(BF16)
            copy = far_copy(mix_send.at[f], mix_recv, mix_ssem, mix_rsem, f, far_chunk(f))
            copy.start()
            pending.append(copy.wait_send)

        for offset in ARRIVAL:
            urgent.append(lambda offset=offset: group_back(offset))
        urgent.append(lambda: keep_own(fret_send.at[f], fret_recv.at[f]))
        mixing.append(mix_far)
        later.append(lambda: wait_recv(blocks_of(fret_send.at[f], DP - 1), fret_ssem.at[f]))

    urgent, mixing = [], []
    for f in range(len(FAR)):
        give_back(f)
    chores.extend(urgent)
    chores.append(lambda: send_pages(1 + EARLY + MIDDLE, DP))
    chores.extend(mixing)
    for j in range(MESSAGES):
        distance = RING - j // SUBS
        offset = RETURN_ORDER[j % SUBS]
        for way in range(2):
            chunk = lax.rem(t + (distance if way == 0 else TP - distance), TP)
            if j % SUBS == 0:
                expert_out(chunk)
            value = ybuf[chunk, rows_at(offset), :]
            if j >= SUBS:
                wait_recv(recvs[way].at[j - SUBS], red_rsem.at[way, j - SUBS])
                value = value + recvs[way][j - SUBS].astype(F32)
            sends[way][j] = value.astype(BF16)
            send_red(way, j)
        if j >= 1 and len(chores) > 1:
            chore()
            if len(chores) > 1:
                chore()
        elif j == MESSAGES - 1:
            chore()
    expert_out(t)
    while chores:
        chore()
    pending.extend(later)
    finish()

    for position, offset in enumerate(RETURN_ORDER):
        value = ybuf[t, rows_at(offset), :]
        for way in range(2):
            j = MESSAGES - SUBS + position
            wait_recv(recvs[way].at[j], red_rsem.at[way, j])
            value = value + recvs[way][j].astype(F32)
        value = value.astype(BF16)
        back = dot(pick_out[0], value[:, :WIDE]) + dot(pick_out[1], value[:, WIDE:])
        rows = pl.ds(pl.multiple_of(group_at(offset) * GROUP_ROWS, GROUP_ROWS), GROUP_ROWS)
        ret_send[rows, :] = back.astype(BF16)
        send_group(ret_send, ret_recv, ret_ssem, ret_rsem.at[0], offset)
    pending.append(lambda: wait_recv(blocks_of(ret_send, DP - 1), ret_ssem.at[0]))
    keep_own(ret_send, ret_recv)
    finish_pages()
    for f in range(len(FAR)):
        wait_recv(mix_recv.at[f], mix_rsem.at[f])
    wait_recv(blocks_of(ret_recv, DP - 1), ret_rsem.at[0])

    returned = ret_recv[...]
    mixture = dot(gather_top, returned) + dot(gather_rest, returned)
    for h in range(2):
        features = slice(h * WIDE, (h + 1) * WIDE)
        total = state[:, features].astype(F32) + mixture[h * TOKENS : (h + 1) * TOKENS]
        for f in range(len(FAR)):
            total = total + mix_recv[f, :, features].astype(F32)
        for r in range(4):
            layer_out[r, :, features] = total[4 * r : 4 * r + 4].astype(BF16)

    finish()


def layer(*operands):
    smem = pl.BlockSpec(memory_space=pltpu.SMEM)
    vmem = pl.BlockSpec(memory_space=pltpu.VMEM)
    hbm = pl.BlockSpec(memory_space=pltpu.HBM)
    anywhere = pl.BlockSpec(memory_space=pl.ANY)
    dma = pltpu.SemaphoreType.DMA
    return pl.pallas_call(
        layer_kernel,
        out_shape=(
            jax.ShapeDtypeStruct((128, 16, WIDE), BF16),
            jax.ShapeDtypeStruct((128, 16, WIDE), BF16),
            jax.ShapeDtypeStruct((4, 4, PART), BF16),
        ),
        in_specs=[smem] + [hbm] * 14,
        out_specs=(anywhere, anywhere, vmem),
        scratch_shapes=[
            pltpu.VMEM((1, 64), jnp.int32),
            pltpu.VMEM((4, 4, 4096), BF16),
            pltpu.VMEM((4, 4, WIDE), BF16),
            pltpu.VMEM((4, 4, WIDE), BF16),
            pltpu.VMEM((4, 4, PART), BF16),
            pltpu.VMEM((1, PART), F32),
            pltpu.VMEM((4, 4, 8), jnp.int32),
            pltpu.VMEM((4, 4, 8), F32),
            pltpu.VMEM((TOKENS, 4096), F32),
            pltpu.VMEM((TOKENS, PART), F32),
            pltpu.VMEM((2, TOKENS, WIDE), F32),
            pltpu.VMEM((1, 128), jnp.int32),
            pltpu.SMEM((1, 128), jnp.int32),
            pltpu.VMEM((2, SUB_ROWS, GROUP_ROWS), BF16),
            pltpu.VMEM((2, GROUP_ROWS, SUB_ROWS), BF16),
            pltpu.VMEM((ROWS, PART), F32),
            pltpu.VMEM((TOKENS, PART), BF16),
            pltpu.VMEM((len(FAR), TOKENS, PART), BF16),
            pltpu.VMEM((len(FAR), DP * BLOCK, WIDE), BF16),
            pltpu.VMEM((len(FAR), DP * BLOCK, WIDE), BF16),
            pltpu.VMEM((len(FAR), DP * BLOCK, WIDE), BF16),
            pltpu.VMEM((len(FAR), DP * BLOCK, WIDE), BF16),
            pltpu.VMEM((len(FAR), TOKENS, PART), BF16),
            pltpu.VMEM((len(FAR), TOKENS, PART), BF16),
            pltpu.VMEM((65, 16, WIDE), BF16),
            pltpu.VMEM((65, 16, WIDE), BF16),
            pltpu.VMEM((128, 16, WIDE), BF16),
            pltpu.VMEM((128, 16, WIDE), BF16),
            pltpu.VMEM((4096, PART), BF16),
            pltpu.VMEM((192, 4096), BF16),
            pltpu.VMEM((192, 4096), BF16),
            pltpu.VMEM((192, 4096), BF16),
            pltpu.VMEM((TP, 80, HEAD), BF16),
            pltpu.VMEM((TP, 80, HEAD), BF16),
            pltpu.VMEM((HEAD, HEAD), F32),
            pltpu.VMEM((TP, TOKENS, PART), BF16),
            pltpu.VMEM((TOKENS, PART), BF16),
            pltpu.VMEM((DP * BLOCK, WIDE), BF16),
            pltpu.VMEM((DP * BLOCK, WIDE), BF16),
            pltpu.VMEM((TP, ROWS, PART), BF16),
            pltpu.VMEM((TP, 1, 256), F32),
            pltpu.VMEM((ROWS, 192), F32),
            pltpu.VMEM((ROWS, 192), F32),
            pltpu.VMEM((TP, ROWS, PART), F32),
            pltpu.VMEM((MESSAGES, SUB_ROWS, PART), BF16),
            pltpu.VMEM((MESSAGES, SUB_ROWS, PART), BF16),
            pltpu.VMEM((MESSAGES, SUB_ROWS, PART), BF16),
            pltpu.VMEM((MESSAGES, SUB_ROWS, PART), BF16),
            pltpu.VMEM((DP * BLOCK, WIDE), BF16),
            pltpu.VMEM((DP * BLOCK, WIDE), BF16),
            dma((17,)),
            dma((2,)), dma((2,)),
            dma((TP,)), dma((TP,)), dma((TP,)), dma((TP,)),
            dma((1,)), dma((4,)),
            dma((TP,)), dma((TP,)),
            dma((2, MESSAGES)), dma((2, MESSAGES)), dma((2, MESSAGES)), dma((2, MESSAGES)),
            dma((1,)), dma((1,)),
        ] + [dma((len(FAR),))] * 8,
        compiler_params=pltpu.CompilerParams(
            collective_id=0, has_side_effects=True, vmem_limit_bytes=60 * 1024 * 1024
        ),
    )(*operands)


def place_kernel(keys, values, rows, keys_out, values_out, rows_out, kbuf, vbuf, rbuf, sems):
    moves = [(rows, rbuf, rows_out)]
    for i in range(4):
        for src, buf, dst in ((keys, kbuf, keys_out), (values, vbuf, values_out)):
            part = pl.ds(i * 32, 32)
            moves.append((src.at[part], buf.at[part], dst.at[part]))
    loads = [
        pltpu.make_async_copy(src, buf, sems.at[0, i]) for i, (src, buf, _) in enumerate(moves)
    ]
    stores = [
        pltpu.make_async_copy(buf, dst, sems.at[1, i]) for i, (_, buf, dst) in enumerate(moves)
    ]
    for load in loads:
        load.start()
    for load, store in zip(loads, stores):
        load.wait()
        store.start()
    for store in stores:
        store.wait()


def place(*arrays):
    hbm = pl.BlockSpec(memory_space=pltpu.HBM)
    return pl.pallas_call(
        place_kernel,
        out_shape=tuple(jax.ShapeDtypeStruct(a.shape, a.dtype) for a in arrays),
        in_specs=[pl.BlockSpec(memory_space=pl.ANY)] * 3,
        out_specs=(hbm,) * 3,
        scratch_shapes=[pltpu.VMEM(a.shape, a.dtype) for a in arrays]
        + [pltpu.SemaphoreType.DMA((2, 9))],
        compiler_params=pltpu.CompilerParams(vmem_limit_bytes=60 * 1024 * 1024),
    )(*arrays)


def shards(
    cache_keys, cache_values, page_dest, lengths, queries, new_keys, new_values, residual,
    out_weight, norm_gain, expert_ids, gate_probs, w_gate, w_up, w_down,
):
    return place(*layer(
        lengths,
        page_dest.reshape(1, -1),
        queries,
        new_keys,
        new_values,
        residual,
        norm_gain[None, :],
        expert_ids,
        gate_probs,
        cache_keys,
        cache_values,
        out_weight,
        w_gate[0].T,
        w_up[0].T,
        w_down[0],
    ))


def solution(mesh):
    in_specs = (
        P("dp", "tp", None),
        P("dp", "tp", None),
        P("dp", None),
        P("dp"),
        P("dp", None, None),
        P("dp", None, None),
        P("dp", None, None),
        P("dp", None, "tp"),
        P(None, "tp"),
        P("tp"),
        P("dp", None, None),
        P("dp", None, None),
        P("dp", None, "tp"),
        P("dp", None, "tp"),
        P("dp", "tp", None),
    )
    out_specs = (P("dp", "tp", None), P("dp", "tp", None), P("dp", None, "tp"))
    return jax.shard_map(shards, mesh=mesh, in_specs=in_specs, out_specs=out_specs, check_vma=False)
```

```python
import math

import jax
import jax.numpy as jnp
from jax import lax
from jax.experimental import pallas as pl
from jax.experimental.pallas import tpu as pltpu
from jax.sharding import PartitionSpec as P

MESH = pl.DeviceIdType.MESH
F32 = jnp.float32
BF16 = jnp.bfloat16

DP = 32
TP = 8
HEAD = 128
TOKENS = 16
SLOTS = 6
PAD_SLOTS = 8
ROWS = DP * SLOTS
BLOCK = 16
GROUP = 8
GROUP_ROWS = GROUP * BLOCK
PART = 512
WIDE = 256
EPSILON = 1e-06
LOW = -1e30
ARRIVAL = (0, 1, 3, 2)
RETURN_ORDER = (2, 1, 3, 0)
RING = 3
FAR = (4,)
EARLY = 12
MIDDLE = 6
PAGES_A_STEP = 2
SUBS = 4
SUB_ROWS = ROWS // SUBS
MESSAGES = RING * SUBS


def iota(shape, dim):
    return lax.broadcasted_iota(jnp.int32, shape, dim)


def onehot(mask):
    return jnp.where(mask, 1.0, 0.0).astype(BF16)


def dot(a, b):
    return jnp.dot(a, b, preferred_element_type=F32)


def dot_last(a, b):
    return lax.dot_general(a, b, (((1,), (1,)), ((), ())), preferred_element_type=F32)


def split_three(value):
    top = value.astype(BF16).astype(F32)
    rest = value - top
    middle = rest.astype(BF16).astype(F32)
    return top, middle, rest - middle


def layer_kernel(
    lengths, page_dest_in, queries_in, new_keys_in, new_values_in, residual_in, gain_in, ids_in,
    probs_in, keys, values, out_weight, w_gate, w_up, w_down,
    moved_keys, moved_values, layer_out,
    page_dest, queries, new_keys, new_values, residual, gain, ids, probs,
    qrows, idrows, new_rows, inverse_row, inverse, pick_in, pick_out, xwide,
    far_send, far_recv, fdisp_send, fdisp_recv, fret_send, fret_recv, mix_send, mix_recv,
    kbuf, vbuf, ksend, vsend, wo, wg, wu, wd,
    part_send, part_recv, coeff, attended, state,
    disp_send, disp_recv, xbuf, sqbuf, gate_acc, up_acc, ybuf,
    lsend, rsend, lrecv, rrecv, ret_send, ret_recv,
    local_sem, page_send_sem, page_recv_sem, part_ssem, part_rsem, att_ssem, att_rsem,
    disp_ssem, disp_rsem, sq_ssem, sq_rsem, ring_ssem, ring_rsem, red_ssem, red_rsem,
    ret_ssem, ret_rsem,
    far_ssem, far_rsem, fdisp_ssem, fdisp_rsem, fret_ssem, fret_rsem, mix_ssem, mix_rsem,
):
    me = lax.axis_index("dp")
    t = lax.axis_index("tp")

    def local(src, dst, i):
        return pltpu.make_async_copy(src, dst, local_sem.at[i])

    small = [
        local(src, dst, 8 + i)
        for i, (src, dst) in enumerate((
            (page_dest_in, page_dest), (queries_in, queries), (new_keys_in, new_keys),
            (new_values_in, new_values), (residual_in, residual), (gain_in, gain),
            (ids_in, ids), (probs_in, probs),
        ))
    ]
    loads = [
        local(keys, kbuf.at[pl.ds(0, 64)], 0),
        local(values, vbuf.at[pl.ds(0, 64)], 1),
        local(out_weight, wo, 2),
        local(w_gate, wg, 3),
        local(w_up, wu, 4),
        local(w_down, wd, 5),
    ]
    for load in small + loads[:2]:
        load.start()

    barrier = pltpu.get_barrier_semaphore()

    for d in range(1, TP):
        pl.semaphore_signal(
            barrier, inc=1, device_id=(me, lax.rem(t + d, TP)), device_id_type=MESH
        )

    for d in range(1, DP):
        pl.semaphore_signal(
            barrier, inc=1, device_id=(lax.rem(me + d, DP), t), device_id_type=MESH
        )

    kbuf[64] = jnp.zeros((16, WIDE), BF16)
    vbuf[64] = jnp.zeros((16, WIDE), BF16)
    for load in small:
        load.wait()

    def rows_together(ref, scratch):
        for r in range(4):
            scratch[4 * r : 4 * r + 4, : ref.shape[2]] = ref[r].astype(F32)
        return scratch[:, : ref.shape[2]]

    rows_together(new_keys, new_rows.at[0])
    rows_together(new_values, new_rows.at[1])
    residual_rows = rows_together(residual, idrows)
    rows_together(queries, qrows)

    dest = jnp.broadcast_to(page_dest[...], (64, 64))
    page_row = iota((64, 64), 0)
    page_col = iota((64, 64), 1)
    dest_of = jnp.sum(jnp.where(page_row == page_col, dest, 0), axis=1, keepdims=True)
    earlier = (dest == dest_of) & (page_col < page_row)
    within = jnp.sum(jnp.where(earlier, 1, 0), axis=1, keepdims=True)
    hit = dest_of * 4 + within == iota((64, 128), 1)
    number = iota((64, 128), 0) - 64
    inverse_row[...] = 64 + jnp.sum(jnp.where(hit, number, 0), axis=0, keepdims=True)
    to_scalars = local(inverse_row, inverse, 16)
    to_scalars.start()

    loads[0].wait()
    loads[1].wait()
    for load in loads[2:]:
        load.start()

    row = iota((256, 256), 0)
    col = iota((256, 256), 1)
    perm = onehot(col == ((row >> 2) & 15) * 16 + (row >> 6) * 4 + (row & 3))
    perm_back = onehot(col == ((row >> 2) & 3) * 64 + (row >> 4) * 4 + (row & 3))
    scale = 1.0 / math.sqrt(HEAD)
    lane = iota((64, 256), 1)
    position = (lane >> 4) * 128 + t * 16 + (lane & 15)
    frow = iota((256, TOKENS), 0)
    fcol = iota((256, TOKENS), 1)
    fvisible = ((fcol >> 2) == (frow >> 6)) & ((fcol & 3) <= (frow & 3)) & (t == 0)
    stat_lane = iota((256, HEAD), 1)

    def part_copy(d):
        dest = lax.rem(t + d, TP)
        return pltpu.make_async_remote_copy(
            src_ref=part_send.at[dest],
            dst_ref=part_recv.at[t],
            send_sem=part_ssem.at[d],
            recv_sem=part_rsem.at[t],
            device_id=(me, dest),
            device_id_type=MESH,
        )

    def attend(k):
        cols = pl.ds(pl.multiple_of(k * HEAD, HEAD), HEAD)
        q_rows = jnp.concatenate(
            [
                qrows[:, pl.ds(pl.multiple_of((k * 16 + g) * HEAD, HEAD), HEAD)]
                for g in range(16)
            ],
            axis=0,
        )
        q_rows = dot(perm, q_rows.astype(BF16)).astype(BF16)
        fresh_k = new_rows[0, :, cols].astype(BF16)
        fresh_v = new_rows[1, :, cols].astype(BF16)
        scores = []
        for r in range(4):
            k_r = kbuf[16 * r : 16 * r + 16, :, cols].reshape(256, HEAD)
            score = dot_last(q_rows[64 * r : 64 * r + 64], k_r) * scale
            scores.append(jnp.where(position < lengths[r], score, LOW))
        scores = jnp.concatenate(scores, axis=0)
        fscores = jnp.where(fvisible, dot_last(q_rows, fresh_k) * scale, LOW)
        top = jnp.maximum(
            jnp.max(scores, axis=1, keepdims=True), jnp.max(fscores, axis=1, keepdims=True)
        )
        weights = jnp.exp(scores - top)
        fweights = jnp.exp(fscores - top)
        total = jnp.sum(weights, axis=1, keepdims=True) + jnp.sum(fweights, axis=1, keepdims=True)
        weights = weights.astype(BF16)
        accs = [
            dot(
                weights[64 * r : 64 * r + 64],
                vbuf[16 * r : 16 * r + 16, :, cols].reshape(256, HEAD),
            )
            for r in range(4)
        ]
        acc = jnp.concatenate(accs, axis=0) + dot(fweights.astype(BF16), fresh_v)
        acc = dot(perm_back, acc.astype(BF16)).astype(BF16)
        stats = jnp.zeros((256, HEAD), F32)
        for i, piece in enumerate(split_three(top) + split_three(total)):
            stats = jnp.where(stat_lane == i, piece, stats)
        stats = jnp.transpose(stats)[0:16].astype(BF16)
        stats = dot(stats, perm).astype(BF16)
        for q in range(4):
            part_send[k * 4 + q, 0:64] = acc[64 * q : 64 * q + 64]
            part_send[k * 4 + q, 64:80] = stats[:, 128 * (q >> 1) : 128 * (q >> 1) + 128]

    far = 1 - (t >> 2)
    attend(far)
    pl.semaphore_wait(barrier, DP - 1 + TP - 1)
    mine_at = t & 3
    for q in range(4):
        part_copy(lax.rem(far * 4 + q + TP - t, TP)).start()
    attend(1 - far)
    for q in range(1, 4):
        part_copy(lax.rem((1 - far) * 4 + ((mine_at + q) & 3) + TP - t, TP)).start()

    def wait_recv(ref, sem):
        pltpu.make_async_copy(ref, ref, sem).wait()

    pending = []

    def finish():
        for wait in pending:
            wait()
        pending.clear()

    def finish_parts():
        for d in range(1, TP):
            part_copy(d).wait_send()

    pending.append(finish_parts)
    part_recv[t] = part_send[t]

    to_scalars.wait()

    @pl.loop(0, 128, unroll=8)
    def _(slot):
        page = jnp.clip(inverse[0, slot], 0, 64)
        ksend[slot] = kbuf[page]
        vsend[slot] = vbuf[page]

    begin = 11 * (me & 1) + 5 * ((me >> 1) & 3) + 8 * (me >> 3)

    def page_copy(which, d):
        dest = lax.rem(me + 1 + lax.rem(d + begin, DP - 1), DP)
        src, dst = ((ksend, moved_keys), (vsend, moved_values))[which]
        return pltpu.make_async_remote_copy(
            src_ref=src.at[pl.ds(dest * 4, 4)],
            dst_ref=dst.at[pl.ds(me * 4, 4)],
            send_sem=page_send_sem.at[which],
            recv_sem=page_recv_sem.at[which],
            device_id=(dest, t),
            device_id_type=MESH,
        )

    own_k = local(ksend.at[pl.ds(me * 4, 4)], moved_keys.at[pl.ds(me * 4, 4)], 6)
    own_v = local(vsend.at[pl.ds(me * 4, 4)], moved_values.at[pl.ds(me * 4, 4)], 7)
    def finish_pages():
        own_k.wait()
        own_v.wait()

        others = pl.ds(0, 4 * (DP - 1))
        for which, ref in enumerate((moved_keys, moved_values)):
            wait_recv(ref.at[others], page_recv_sem.at[which])
            wait_recv(ref.at[others], page_send_sem.at[which])

    def send_pages(first, last):
        @pl.loop(first, last)
        def _(d):
            page_copy(0, d).start()
            page_copy(1, d).start()

    own_k.start()
    own_v.start()
    send_pages(1, 1 + EARLY)

    for d in range(1, TP):
        src = lax.rem(t + d, TP)
        wait_recv(part_recv.at[src], part_rsem.at[src])
    tops, sums = [], []
    for s in range(TP):
        stat = part_recv[s, 64:80].astype(F32)
        tops.append(stat[0:1] + stat[1:2] + stat[2:3])
        sums.append(stat[3:4] + stat[4:5] + stat[5:6])
    tops = jnp.concatenate(tops, axis=0)
    sums = jnp.concatenate(sums, axis=0)
    scales = jnp.exp(tops - jnp.max(tops, axis=0, keepdims=True))
    scales = scales / jnp.sum(scales * sums, axis=0, keepdims=True)
    scales = jnp.concatenate([scales, jnp.zeros((120, HEAD), F32)], axis=0)
    coeff[...] = jnp.transpose(scales)
    mine = coeff[pl.ds(pl.multiple_of((t & 1) * 64, 64), 64), :]
    merged = jnp.zeros((64, HEAD), F32)
    for s in range(TP):
        merged = merged + mine[:, s : s + 1] * part_recv[s, 0:64].astype(F32)
    merged = merged.astype(BF16)
    for h in range(4):
        attended[t, :, h * HEAD : (h + 1) * HEAD] = merged[h * 16 : h * 16 + 16]

    def att_copy(d):
        return pltpu.make_async_remote_copy(
            src_ref=attended.at[t],
            dst_ref=attended.at[t],
            send_sem=att_ssem.at[d],
            recv_sem=att_rsem.at[t],
            device_id=(me, lax.rem(t + d, TP)),
            device_id_type=MESH,
        )

    def send_att(d):
        att_copy(d).start()
        pending.append(lambda: att_copy(d).wait_send())

    for d in (4, 3, 5, 2, 6, 1, 7):
        send_att(d)

    named = rows_together(ids, idrows)
    prob = rows_together(probs, idrows)
    expert = iota((TOKENS, DP), 1).astype(F32)
    member = jnp.zeros((TOKENS, DP), F32)
    weight = jnp.zeros((TOKENS, DP), F32)
    for j in range(8):
        same = named[:, j : j + 1] == expert
        member = member + jnp.where(same, 1.0, 0.0)
        weight = weight + jnp.where(same, prob[:, j : j + 1], 0.0)
    member = member.astype(BF16)
    below = onehot(iota((TOKENS, TOKENS), 1) < iota((TOKENS, TOKENS), 0))
    rank = dot(below, member).astype(BF16)
    lane_expert = onehot((iota((DP, DP * BLOCK), 1) >> 4) == iota((DP, DP * BLOCK), 0))
    lane = iota((TOKENS, DP * BLOCK), 1)
    chosen = jnp.where(
        dot(rank, lane_expert) == (lane & 7).astype(F32), dot(member, lane_expert), 0.0
    )
    first = jnp.where((lane & 8) == 0, chosen, 0.0)
    scatter_back = jnp.concatenate([first, chosen - first], axis=0)
    scatter = jnp.transpose(scatter_back).astype(BF16)
    weight_top = weight.astype(BF16)
    weight_rest = (weight - weight_top.astype(F32)).astype(BF16)
    gather_top, gather_rest = [
        jnp.concatenate([part, part], axis=0) for part in (
            dot(weight_top, lane_expert), dot(weight_rest, lane_expert))
    ]
    gather_top = (gather_top * scatter_back).astype(BF16)
    gather_rest = (gather_rest * scatter_back).astype(BF16)

    prow = iota((SUB_ROWS, GROUP_ROWS), 0)
    pcol = iota((SUB_ROWS, GROUP_ROWS), 1)
    source = (prow * 683) >> 12
    place = source * BLOCK + prow - source * SLOTS
    rrow = iota((GROUP_ROWS, SUB_ROWS), 0)
    rcol = iota((GROUP_ROWS, SUB_ROWS), 1)
    rslot = rrow & 7
    rplace = (rrow >> 4) * SLOTS + rslot
    for h in range(2):
        pick_in[h] = onehot(pcol == place + h * PAD_SLOTS)
        pick_out[h] = onehot((rcol == rplace) & (rslot < SLOTS) & (((rrow >> 3) & 1) == h))

    loads[2].wait()

    def project(src):
        return dot(attended[src], wo[pl.ds(pl.multiple_of(src * PART, PART), PART), :])

    projected = project(t)
    for d in (1, 7, 2, 6, 3, 5, 4):
        src = lax.rem(t + d, TP)
        wait_recv(attended.at[src], att_rsem.at[src])
        projected = projected + project(src)
    layer_state = (residual_rows + projected).astype(BF16)
    state[...] = layer_state

    stacked = jnp.concatenate([layer_state[:, :WIDE], layer_state[:, WIDE:]], axis=0)
    disp_send[...] = dot(scatter, stacked).astype(BF16)

    def block_of(ref, rank):
        return ref.at[pl.ds(pl.multiple_of(rank * BLOCK, BLOCK), BLOCK)]

    group = me >> 3

    def group_at(offset):
        return (group + offset) & 3

    def blocks_of(ref, count):
        return ref.at[pl.ds(0, count * BLOCK)]

    def send_group(send, recv, ssem, rsem, offset):
        for i in range(1 if offset == 0 else 0, GROUP):
            dest = group_at(offset) * GROUP + ((me + i) & 7)
            pltpu.make_async_remote_copy(
                src_ref=block_of(send, dest),
                dst_ref=block_of(recv, me),
                send_sem=ssem.at[0],
                recv_sem=rsem,
                device_id=(dest, t),
                device_id_type=MESH,
            ).start()

    def keep_own(send, recv):
        block = pl.ds(pl.multiple_of(me * BLOCK, BLOCK), BLOCK)
        recv[block, :] = send[block, :]

    for offset in ARRIVAL:
        send_group(disp_send, disp_recv, disp_ssem, disp_rsem.at[group], offset)
    pending.append(lambda: wait_recv(blocks_of(disp_send, DP - 1), disp_ssem.at[0]))
    keep_own(disp_send, disp_recv)

    def far_copy(send, recv, ssem, rsem, f, dest):
        return pltpu.make_async_remote_copy(
            src_ref=send,
            dst_ref=recv.at[f],
            send_sem=ssem.at[f],
            recv_sem=rsem.at[f],
            device_id=(me, dest),
            device_id_type=MESH,
        )

    far_send[...] = (layer_state.astype(F32) * gain[...]).astype(BF16)

    def start_far(f):
        copy = far_copy(
            far_send, far_recv, far_ssem, far_rsem, f, lax.rem(t + FAR[f], TP)
        )
        copy.start()
        pending.append(copy.wait_send)

    for f in range(len(FAR)):
        start_far(f)

    def far_chunk(f):
        return lax.rem(t + TP - FAR[f], TP)

    chores = []

    def spread(send, recv, ssem, rsem, f):
        for offset in ARRIVAL:
            chores.append(
                lambda offset=offset: send_group(
                    send.at[f], recv.at[f], ssem.at[pl.ds(f, 1)], rsem.at[f], offset
                )
            )
        chores.append(lambda: keep_own(send.at[f], recv.at[f]))

    def pass_on(f):
        def scatter_far():
            wait_recv(far_recv.at[f], far_rsem.at[f])
            rows = far_recv[f]
            rows = jnp.concatenate([rows[:, :WIDE], rows[:, WIDE:]], axis=0)
            fdisp_send[f] = dot(scatter, rows).astype(BF16)

        chores.append(scatter_far)
        spread(fdisp_send, fdisp_recv, fdisp_ssem, fdisp_rsem, f)
        later.append(lambda: wait_recv(blocks_of(fdisp_send.at[f], DP - 1), fdisp_ssem.at[f]))

    later = []
    for f in range(len(FAR)):
        pass_on(f)
    page_chores = []
    for first in range(1 + EARLY, 1 + EARLY + MIDDLE, PAGES_A_STEP):
        page_chores.append(lambda first=first: send_pages(first, first + PAGES_A_STEP))
    chores.extend(page_chores)

    def chore():
        if chores:
            chores.pop(0)()

    def rows_at(offset):
        return pl.ds(pl.multiple_of(group_at(offset) * SUB_ROWS, SUB_ROWS), SUB_ROWS)

    toward = (lax.rem(t + 1, TP), lax.rem(t + TP - 1, TP))

    def ring_piece(way, i, step):
        chunk = lax.rem(t + (TP - step if way == 0 else step), TP)
        return xbuf.at[chunk, rows_at(ARRIVAL[i % SUBS])]

    def ring_copy(way, i):
        piece = ring_piece(way, i, i // SUBS)
        return pltpu.make_async_remote_copy(
            src_ref=piece,
            dst_ref=piece,
            send_sem=ring_ssem.at[way, i],
            recv_sem=ring_rsem.at[way, i],
            device_id=(me, toward[way]),
            device_id_type=MESH,
        )

    def ring_wait(way, i):
        wait_recv(ring_piece(way, i, i // SUBS + 1), ring_rsem.at[way, i])

    def expert_in(chunk, first=False):
        x = xbuf[chunk]
        features = pl.ds(pl.multiple_of(chunk * PART, PART), PART)
        gate_part = dot_last(x, wg[:, features])
        up_part = dot_last(x, wu[:, features])
        if first:
            gate_acc[...] = gate_part
            up_acc[...] = up_part
        else:
            gate_acc[...] += gate_part
            up_acc[...] += up_part

    def send_ring(way, i):
        ring_copy(way, i).start()
        pending.append(lambda: ring_copy(way, i).wait_send())

    for at, offset in enumerate(ARRIVAL):
        count = GROUP - 1 if offset == 0 else GROUP
        wait_recv(blocks_of(disp_recv, count), disp_rsem.at[group_at(offset)])
        arrived = disp_recv[
            pl.ds(pl.multiple_of(group_at(offset) * GROUP_ROWS, GROUP_ROWS), GROUP_ROWS), :
        ]
        for h in range(2):
            features = slice(h * WIDE, (h + 1) * WIDE)
            piece = dot(pick_in[h], arrived)
            xwide[rows_at(offset), features] = piece
            xbuf[t, rows_at(offset), features] = (piece * gain[:, features]).astype(BF16)
        for way in range(2):
            send_ring(way, at)

    square = jnp.sum(xwide[...] * xwide[...], axis=1, keepdims=True)
    square = jnp.concatenate([square, jnp.zeros((256 - ROWS, 1), F32)], axis=0)
    sqbuf[t] = jnp.transpose(jnp.broadcast_to(square, (256, HEAD)))[0:1]

    def sq_copy(d):
        return pltpu.make_async_remote_copy(
            src_ref=sqbuf.at[t],
            dst_ref=sqbuf.at[t],
            send_sem=sq_ssem.at[d],
            recv_sem=sq_rsem.at[t],
            device_id=(me, lax.rem(t + d, TP)),
            device_id_type=MESH,
        )

    def send_sq(d):
        sq_copy(d).start()
        pending.append(lambda: sq_copy(d).wait_send())

    for d in range(1, TP):
        send_sq(d)

    loads[3].wait()
    loads[4].wait()
    expert_in(t, first=True)
    for i in range(MESSAGES):
        for way in range(2):
            ring_wait(way, i)
            if i + SUBS < MESSAGES:
                send_ring(way, i + SUBS)
        chore()
        if i % SUBS == SUBS - 1:
            expert_in(lax.rem(t + TP - (i // SUBS + 1), TP))
            expert_in(lax.rem(t + i // SUBS + 1, TP))
    while len(chores) > len(page_chores):
        chore()
    for f in range(len(FAR)):
        wait_recv(blocks_of(fdisp_recv.at[f], DP - 1), fdisp_rsem.at[f])
        for g in range(4):
            arrived = fdisp_recv[f, g * GROUP_ROWS : (g + 1) * GROUP_ROWS]
            for h in range(2):
                xbuf[
                    far_chunk(f), g * SUB_ROWS : (g + 1) * SUB_ROWS, h * WIDE : (h + 1) * WIDE
                ] = dot(pick_in[h], arrived).astype(BF16)
        expert_in(far_chunk(f))

    for d in range(1, TP):
        src = lax.rem(t + d, TP)
        wait_recv(sqbuf.at[src], sq_rsem.at[src])
    total = sqbuf[0]
    for s in range(1, TP):
        total = total + sqbuf[s]
    inv_norm = lax.rsqrt(total * (1.0 / (TP * PART)) + EPSILON)
    inv_norm = jnp.transpose(jnp.broadcast_to(inv_norm, (HEAD, 256)))[0:ROWS, 0:1]
    gate_part = gate_acc[...] * inv_norm
    up_part = up_acc[...] * inv_norm
    hidden = (gate_part / (1.0 + jnp.exp(-gate_part)) * up_part).astype(BF16)

    loads[5].wait()
    sends = (rsend, lsend)
    recvs = (rrecv, lrecv)

    def expert_out(chunk):
        ybuf[chunk] = dot(hidden, wd[:, pl.ds(pl.multiple_of(chunk * PART, PART), PART)])

    def red_copy(way, j):
        return pltpu.make_async_remote_copy(
            src_ref=sends[way].at[j],
            dst_ref=recvs[way].at[j],
            send_sem=red_ssem.at[way, j],
            recv_sem=red_rsem.at[way, j],
            device_id=(me, toward[way]),
            device_id_type=MESH,
        )

    def send_red(way, j):
        red_copy(way, j).start()
        pending.append(lambda: red_copy(way, j).wait_send())

    def give_back(f):
        def group_back(offset):
            if offset == ARRIVAL[0]:
                expert_out(far_chunk(f))
            value = ybuf[far_chunk(f), rows_at(offset), :].astype(BF16)
            back = dot(pick_out[0], value[:, :WIDE]) + dot(pick_out[1], value[:, WIDE:])
            rows = pl.ds(pl.multiple_of(group_at(offset) * GROUP_ROWS, GROUP_ROWS), GROUP_ROWS)
            fret_send[f, rows, :] = back.astype(BF16)
            send_group(
                fret_send.at[f], fret_recv.at[f], fret_ssem.at[pl.ds(f, 1)], fret_rsem.at[f], offset
            )

        def mix_far():
            wait_recv(blocks_of(fret_recv.at[f], DP - 1), fret_rsem.at[f])
            returned = fret_recv[f]
            mixture = dot(gather_top, returned) + dot(gather_rest, returned)
            for h in range(2):
                mix_send[f, :, h * WIDE : (h + 1) * WIDE] = mixture[
                    h * TOKENS : (h + 1) * TOKENS
                ].astype(BF16)
            copy = far_copy(mix_send.at[f], mix_recv, mix_ssem, mix_rsem, f, far_chunk(f))
            copy.start()
            pending.append(copy.wait_send)

        for offset in ARRIVAL:
            urgent.append(lambda offset=offset: group_back(offset))
        urgent.append(lambda: keep_own(fret_send.at[f], fret_recv.at[f]))
        mixing.append(mix_far)
        later.append(lambda: wait_recv(blocks_of(fret_send.at[f], DP - 1), fret_ssem.at[f]))

    urgent, mixing = [], []
    for f in range(len(FAR)):
        give_back(f)
    chores.extend(urgent)
    chores.append(lambda: send_pages(1 + EARLY + MIDDLE, DP))
    chores.extend(mixing)
    for j in range(MESSAGES):
        distance = RING - j // SUBS
        offset = RETURN_ORDER[j % SUBS]
        for way in range(2):
            chunk = lax.rem(t + (distance if way == 0 else TP - distance), TP)
            if j % SUBS == 0:
                expert_out(chunk)
            value = ybuf[chunk, rows_at(offset), :]
            if j >= SUBS:
                wait_recv(recvs[way].at[j - SUBS], red_rsem.at[way, j - SUBS])
                value = value + recvs[way][j - SUBS].astype(F32)
            sends[way][j] = value.astype(BF16)
            send_red(way, j)
        if j >= 1 and len(chores) > 1:
            chore()
            if len(chores) > 1:
                chore()
        elif j == MESSAGES - 1:
            chore()
    expert_out(t)
    while chores:
        chore()
    pending.extend(later)

    for position, offset in enumerate(RETURN_ORDER):
        value = ybuf[t, rows_at(offset), :]
        for way in range(2):
            j = MESSAGES - SUBS + position
            wait_recv(recvs[way].at[j], red_rsem.at[way, j])
            value = value + recvs[way][j].astype(F32)
        value = value.astype(BF16)
        back = dot(pick_out[0], value[:, :WIDE]) + dot(pick_out[1], value[:, WIDE:])
        rows = pl.ds(pl.multiple_of(group_at(offset) * GROUP_ROWS, GROUP_ROWS), GROUP_ROWS)
        ret_send[rows, :] = back.astype(BF16)
        send_group(ret_send, ret_recv, ret_ssem, ret_rsem.at[0], offset)
    keep_own(ret_send, ret_recv)
    finish()
    pending.append(lambda: wait_recv(blocks_of(ret_send, DP - 1), ret_ssem.at[0]))
    finish_pages()
    for f in range(len(FAR)):
        wait_recv(mix_recv.at[f], mix_rsem.at[f])
    wait_recv(blocks_of(ret_recv, DP - 1), ret_rsem.at[0])

    returned = ret_recv[...]
    mixture = dot(gather_top, returned) + dot(gather_rest, returned)
    for h in range(2):
        features = slice(h * WIDE, (h + 1) * WIDE)
        total = state[:, features].astype(F32) + mixture[h * TOKENS : (h + 1) * TOKENS]
        for f in range(len(FAR)):
            total = total + mix_recv[f, :, features].astype(F32)
        for r in range(4):
            layer_out[r, :, features] = total[4 * r : 4 * r + 4].astype(BF16)

    finish()


def layer(*operands):
    smem = pl.BlockSpec(memory_space=pltpu.SMEM)
    vmem = pl.BlockSpec(memory_space=pltpu.VMEM)
    hbm = pl.BlockSpec(memory_space=pltpu.HBM)
    anywhere = pl.BlockSpec(memory_space=pl.ANY)
    dma = pltpu.SemaphoreType.DMA
    return pl.pallas_call(
        layer_kernel,
        out_shape=(
            jax.ShapeDtypeStruct((128, 16, WIDE), BF16),
            jax.ShapeDtypeStruct((128, 16, WIDE), BF16),
            jax.ShapeDtypeStruct((4, 4, PART), BF16),
        ),
        in_specs=[smem] + [hbm] * 14,
        out_specs=(anywhere, anywhere, vmem),
        scratch_shapes=[
            pltpu.VMEM((1, 64), jnp.int32),
            pltpu.VMEM((4, 4, 4096), BF16),
            pltpu.VMEM((4, 4, WIDE), BF16),
            pltpu.VMEM((4, 4, WIDE), BF16),
            pltpu.VMEM((4, 4, PART), BF16),
            pltpu.VMEM((1, PART), F32),
            pltpu.VMEM((4, 4, 8), jnp.int32),
            pltpu.VMEM((4, 4, 8), F32),
            pltpu.VMEM((TOKENS, 4096), F32),
            pltpu.VMEM((TOKENS, PART), F32),
            pltpu.VMEM((2, TOKENS, WIDE), F32),
            pltpu.VMEM((1, 128), jnp.int32),
            pltpu.SMEM((1, 128), jnp.int32),
            pltpu.VMEM((2, SUB_ROWS, GROUP_ROWS), BF16),
            pltpu.VMEM((2, GROUP_ROWS, SUB_ROWS), BF16),
            pltpu.VMEM((ROWS, PART), F32),
            pltpu.VMEM((TOKENS, PART), BF16),
            pltpu.VMEM((len(FAR), TOKENS, PART), BF16),
            pltpu.VMEM((len(FAR), DP * BLOCK, WIDE), BF16),
            pltpu.VMEM((len(FAR), DP * BLOCK, WIDE), BF16),
            pltpu.VMEM((len(FAR), DP * BLOCK, WIDE), BF16),
            pltpu.VMEM((len(FAR), DP * BLOCK, WIDE), BF16),
            pltpu.VMEM((len(FAR), TOKENS, PART), BF16),
            pltpu.VMEM((len(FAR), TOKENS, PART), BF16),
            pltpu.VMEM((65, 16, WIDE), BF16),
            pltpu.VMEM((65, 16, WIDE), BF16),
            pltpu.VMEM((128, 16, WIDE), BF16),
            pltpu.VMEM((128, 16, WIDE), BF16),
            pltpu.VMEM((4096, PART), BF16),
            pltpu.VMEM((192, 4096), BF16),
            pltpu.VMEM((192, 4096), BF16),
            pltpu.VMEM((192, 4096), BF16),
            pltpu.VMEM((TP, 80, HEAD), BF16),
            pltpu.VMEM((TP, 80, HEAD), BF16),
            pltpu.VMEM((HEAD, HEAD), F32),
            pltpu.VMEM((TP, TOKENS, PART), BF16),
            pltpu.VMEM((TOKENS, PART), BF16),
            pltpu.VMEM((DP * BLOCK, WIDE), BF16),
            pltpu.VMEM((DP * BLOCK, WIDE), BF16),
            pltpu.VMEM((TP, ROWS, PART), BF16),
            pltpu.VMEM((TP, 1, 256), F32),
            pltpu.VMEM((ROWS, 192), F32),
            pltpu.VMEM((ROWS, 192), F32),
            pltpu.VMEM((TP, ROWS, PART), F32),
            pltpu.VMEM((MESSAGES, SUB_ROWS, PART), BF16),
            pltpu.VMEM((MESSAGES, SUB_ROWS, PART), BF16),
            pltpu.VMEM((MESSAGES, SUB_ROWS, PART), BF16),
            pltpu.VMEM((MESSAGES, SUB_ROWS, PART), BF16),
            pltpu.VMEM((DP * BLOCK, WIDE), BF16),
            pltpu.VMEM((DP * BLOCK, WIDE), BF16),
            dma((17,)),
            dma((2,)), dma((2,)),
            dma((TP,)), dma((TP,)), dma((TP,)), dma((TP,)),
            dma((1,)), dma((4,)),
            dma((TP,)), dma((TP,)),
            dma((2, MESSAGES)), dma((2, MESSAGES)), dma((2, MESSAGES)), dma((2, MESSAGES)),
            dma((1,)), dma((1,)),
        ] + [dma((len(FAR),))] * 8,
        compiler_params=pltpu.CompilerParams(
            collective_id=0, has_side_effects=True, vmem_limit_bytes=60 * 1024 * 1024
        ),
    )(*operands)


def place_kernel(keys, values, rows, keys_out, values_out, rows_out, kbuf, vbuf, rbuf, sems):
    moves = [(rows, rbuf, rows_out)]
    for i in range(4):
        for src, buf, dst in ((keys, kbuf, keys_out), (values, vbuf, values_out)):
            part = pl.ds(i * 32, 32)
            moves.append((src.at[part], buf.at[part], dst.at[part]))
    loads = [
        pltpu.make_async_copy(src, buf, sems.at[0, i]) for i, (src, buf, _) in enumerate(moves)
    ]
    stores = [
        pltpu.make_async_copy(buf, dst, sems.at[1, i]) for i, (_, buf, dst) in enumerate(moves)
    ]
    for load in loads:
        load.start()
    for load, store in zip(loads, stores):
        load.wait()
        store.start()
    for store in stores:
        store.wait()


def place(*arrays):
    hbm = pl.BlockSpec(memory_space=pltpu.HBM)
    return pl.pallas_call(
        place_kernel,
        out_shape=tuple(jax.ShapeDtypeStruct(a.shape, a.dtype) for a in arrays),
        in_specs=[pl.BlockSpec(memory_space=pl.ANY)] * 3,
        out_specs=(hbm,) * 3,
        scratch_shapes=[pltpu.VMEM(a.shape, a.dtype) for a in arrays]
        + [pltpu.SemaphoreType.DMA((2, 9))],
        compiler_params=pltpu.CompilerParams(vmem_limit_bytes=60 * 1024 * 1024),
    )(*arrays)


def shards(
    cache_keys, cache_values, page_dest, lengths, queries, new_keys, new_values, residual,
    out_weight, norm_gain, expert_ids, gate_probs, w_gate, w_up, w_down,
):
    return place(*layer(
        lengths,
        page_dest.reshape(1, -1),
        queries,
        new_keys,
        new_values,
        residual,
        norm_gain[None, :],
        expert_ids,
        gate_probs,
        cache_keys,
        cache_values,
        out_weight,
        w_gate[0].T,
        w_up[0].T,
        w_down[0],
    ))


def solution(mesh):
    in_specs = (
        P("dp", "tp", None),
        P("dp", "tp", None),
        P("dp", None),
        P("dp"),
        P("dp", None, None),
        P("dp", None, None),
        P("dp", None, None),
        P("dp", None, "tp"),
        P(None, "tp"),
        P("tp"),
        P("dp", None, None),
        P("dp", None, None),
        P("dp", None, "tp"),
        P("dp", None, "tp"),
        P("dp", "tp", None),
    )
    out_specs = (P("dp", "tp", None), P("dp", "tp", None), P("dp", None, "tp"))
    return jax.shard_map(shards, mesh=mesh, in_specs=in_specs, out_specs=out_specs, check_vma=False)
```
